32 devices in a mesh: ty: 4 (over x, core), tx: 8 (over z, y).
Axes of the slice: x: 2, y: 2, z: 4, core: 2. Of those that a mesh axis runs over, the one named last changes fastest.
Arguments:
- spectrum: float32 [2, 2048, 4096], P(None, 'ty', 'tx')
- measured: float32 [32, 256, 256], P(('ty', 'tx')), may hold values from 0.5 to 6
- pupil_mask: int32 [256, 256], replicated, may hold values 0 or 1
- led_count: int32 [32], replicated, may hold values from 4 to 8, as said below
- led_owner: int32 [32, 8], replicated, may hold values from 0 to 7, as said below
- led_offset: int32 [32, 8, 2], replicated, may hold values from 0 to 256
Outputs:
- spectrum_step: float32 [2, 2048, 4096], P(None, 'ty', 'tx')
- cg_residual: float32 [2, 2048, 4096], P(None, 'ty', 'tx')
The draws below stay inside these ranges and needn't reach their ends.
Inputs may be any that keep to these rules, and one draw needn't show every extreme that they name: Capture c lights the LEDs of slots 0 to led_count[c] - 1; some capture lights 8 in every draw. `led_owner`: for capture c, taken on device (c // 8, c % 8) of the mesh (ty, tx), slot t names the column of the tile in tile row c // 8 that holds the slot's block. The live slots of one capture name distinct tiles. No tile holds the blocks of more than 8 live slots over the captures of its tile row, and in every tile row some tile holds exactly 8. `led_offset`: every block lies inside the tile named by led_owner.
All inputs are finite; a program needn't handle non-finite values.
Results may differ from the reference program's by a relative error of at most 0.0003.
Values sent between devices are 32-bit elements; how exact they have to be, the bound alone decides.
No kernel may reach another device: no remote copies, remote signals or barrier semaphores. Data moves between devices by JAX's collectives and lax.ppermute only.
A program may use at most 128 MiB of HBM per device.

```python
import jax
import jax.numpy as jnp
from jax import lax

B = 256
TILE_R = 512
TILE_C = 512
LED_MOST = 8
ITERS = 2
CAPTURES = 32
ROWS_ALL = 2048
COLS_ALL = 4096
N_TY = 4
N_TX = 8


def draw_spectrum(key, part):
    keys = jax.random.split(key, 3)
    base = jax.random.normal(keys[0], (2, ROWS_ALL, COLS_ALL), jnp.float32)
    row_ramp = jnp.exp(jnp.arange(ROWS_ALL, dtype=jnp.float32) * (0.55 / ROWS_ALL))
    col_ramp = jnp.exp(jnp.arange(COLS_ALL, dtype=jnp.float32) * (0.55 / COLS_ALL))
    row_jitter = jnp.exp(jax.random.uniform(keys[1], (ROWS_ALL,), jnp.float32, 0.0, 0.5))
    col_jitter = jnp.exp(jax.random.uniform(keys[2], (COLS_ALL,), jnp.float32, 0.0, 0.5))
    rows_scale = row_ramp * row_jitter
    cols_scale = col_ramp * col_jitter
    return 0.25 * base * rows_scale[None, :, None] * cols_scale[None, None, :]


def led_layout(key):
    count_key = jax.random.fold_in(key, 101)
    place_key = jax.random.fold_in(key, 202)
    tile_key = jax.random.fold_in(key, 303)
    start_key = jax.random.fold_in(key, 404)
    counts = jax.random.randint(count_key, (N_TY, N_TX), 4, LED_MOST + 1)
    columns = jnp.arange(N_TX, dtype=jnp.int32)[None, :]
    place_scores = jax.random.randint(place_key, (N_TY, N_TX), 0, 1 << 20) * N_TX + columns
    tile_scores = jax.random.randint(tile_key, (N_TY, N_TX), 0, 1 << 20) * N_TX + columns
    position = jnp.argsort(jnp.argsort(place_scores, axis=1, stable=True), axis=1, stable=True).astype(jnp.int32)
    tile_order = jnp.argsort(tile_scores, axis=1, stable=True).astype(jnp.int32)
    run_start = jax.random.randint(start_key, (N_TY, 1), 0, N_TX)
    distance = (position - run_start) % N_TX
    counts = jnp.where(distance < LED_MOST, jnp.maximum(counts, LED_MOST - distance), counts)
    slot_ids = jnp.arange(LED_MOST, dtype=jnp.int32)
    lookup = ((position[:, :, None] + slot_ids[None, None, :]) % N_TX).reshape(N_TY, N_TX * LED_MOST)
    owners = jnp.take_along_axis(tile_order, lookup, axis=1)
    return (counts.reshape(CAPTURES).astype(jnp.int32), owners.reshape(CAPTURES, LED_MOST).astype(jnp.int32))


def draw_led_count(key, part):
    return led_layout(key)[0]


def draw_led_owner(key, part):
    return led_layout(key)[1]


def set_ends(values, key, least, top_value):
    extent = values.shape
    index_at = [jax.random.randint(jax.random.fold_in(key, axis), (), 0, extent[axis]) for axis in range(len(extent))]
    values = values.at[tuple(index_at)].set(least)
    longest = extent.index(max(extent))
    index_at[longest] = (index_at[longest] + 1) % extent[longest]
    return values.at[tuple(index_at)].set(top_value)


def block_scale(key, dims, pieces, low, largest):
    def one(axis_at, shards_of):
        heights = jax.random.uniform(jax.random.fold_in(jax.random.fold_in(key, 6), axis_at), (shards_of,), jnp.float32, low / len(pieces), largest / len(pieces))
        return jnp.repeat(jnp.exp(heights), dims[axis_at] // shards_of).reshape((-1,) + (1,) * (len(dims) - axis_at - 1))

    loudness = one(*pieces[0])
    for cut in pieces[1:]:
        loudness = loudness * one(*cut)
    return loudness


def setup_inputs(seed: int = 0) -> dict:
    key_list = jax.random.split(jax.random.key(seed), 7)
    spectrum = draw_spectrum(jax.random.fold_in(key_list[6], 71), 0)
    measured = jnp.clip(0.5 + 5.5 * jax.random.uniform(key_list[1], (CAPTURES, B, B), jnp.float32) ** block_scale(key_list[1], (CAPTURES, B, B), ((0, 32),), -0.2, 0.2), 0.5, 6.0)
    pupil_mask = set_ends((jax.random.randint(key_list[2], (B, B), 0, 4) < 3).astype(jnp.int32), jax.random.fold_in(key_list[2], 1), 0, 1)
    led_count = draw_led_count(jax.random.fold_in(key_list[6], 71), 0)
    led_owner = draw_led_owner(jax.random.fold_in(key_list[6], 71), 0)
    led_offset = set_ends(jax.random.randint(key_list[5], (CAPTURES, LED_MOST, 2), 0, min(TILE_R, TILE_C) - B + 1), jax.random.fold_in(key_list[5], 1), 0, min(TILE_R, TILE_C) - B).astype(jnp.int32)
    return {"spectrum": spectrum, "measured": measured, "pupil_mask": pupil_mask, "led_count": led_count, "led_owner": led_owner, "led_offset": led_offset}


REG = 0.5

def dft_tables(side_len):
    indices = jnp.arange(side_len, dtype=jnp.int32)
    product = indices[:, None] * indices[None, :] % side_len
    angles = product.astype(jnp.float32) * (2.0 * jnp.pi / side_len)
    scale_one = 1.0 / jnp.sqrt(jnp.asarray(side_len, jnp.float32))
    return (jnp.cos(angles) * scale_one, jnp.sin(angles) * scale_one)

def transform(real_part, imag_part, cosine_table, sine_table, orient):
    highest = lax.Precision.HIGHEST
    left_real = jnp.einsum('jk,skl->sjl', cosine_table, real_part, precision=highest) - orient * jnp.einsum('jk,skl->sjl', sine_table, imag_part, precision=highest)
    left_imag = jnp.einsum('jk,skl->sjl', cosine_table, imag_part, precision=highest) + orient * jnp.einsum('jk,skl->sjl', sine_table, real_part, precision=highest)
    out_real = jnp.einsum('sjk,kl->sjl', left_real, cosine_table, precision=highest) - orient * jnp.einsum('sjk,kl->sjl', left_imag, sine_table, precision=highest)
    out_imag = jnp.einsum('sjk,kl->sjl', left_imag, cosine_table, precision=highest) + orient * jnp.einsum('sjk,kl->sjl', left_real, sine_table, precision=highest)
    return (out_real, out_imag)

def laplace(values):
    padded = jnp.pad(values, ((0, 0), (1, 1), (1, 1)))
    neighbours = padded[:, 2:, 1:-1] + padded[:, :-2, 1:-1] + padded[:, 1:-1, 2:] + padded[:, 1:-1, :-2]
    return 4.0 * values - neighbours

def reference(spectrum, measured, pupil_mask, led_count, led_owner, led_offset):
    cosine_table, sine_table = dft_tables(B)
    pupil = pupil_mask.astype(jnp.float32)
    capture_ids = jnp.arange(CAPTURES, dtype=jnp.int32)
    slot_ids = jnp.arange(LED_MOST, dtype=jnp.int32)
    live = (slot_ids[None, :] < led_count[:, None]).astype(jnp.float32).reshape(-1)[:, None, None]
    top_rows = (capture_ids // N_TX * TILE_R)[:, None] + led_offset[:, :, 0]
    left_cols = led_owner * TILE_C + led_offset[:, :, 1]
    top_rows = top_rows.reshape(-1).astype(jnp.int32)
    left_cols = left_cols.reshape(-1).astype(jnp.int32)
    anchor = jnp.zeros((), jnp.int32)

    def extract(values):

        def one_block(row_at, col_at):
            return lax.dynamic_slice(values, (anchor, row_at, col_at), (2, B, B))
        blocks = jax.vmap(one_block)(top_rows, left_cols)
        return (blocks[:, 0] * pupil, blocks[:, 1] * pupil)
    field_real, field_imag = transform(*extract(spectrum), cosine_table, sine_table, 1.0)

    def per_capture(images):
        return lax.optimization_barrier(jnp.sum((images * live).reshape(CAPTURES, LED_MOST, B, B), axis=1))

    def forward(values):
        lin_real, lin_imag = transform(*extract(values), cosine_table, sine_table, 1.0)
        return per_capture(2.0 * (field_real * lin_real + field_imag * lin_imag))

    def adjoint(capture_imgs):
        spread = jnp.repeat(capture_imgs, LED_MOST, axis=0)
        back_real, back_imag = transform(2.0 * field_real * spread, 2.0 * field_imag * spread, cosine_table, sine_table, -1.0)
        contrib = jnp.stack([back_real * pupil * live, back_imag * pupil * live], axis=1)

        def add_block(pair_no, deposit):
            corner = (anchor, top_rows[pair_no], left_cols[pair_no])
            window = lax.dynamic_slice(deposit, corner, (2, B, B))
            return lax.dynamic_update_slice(deposit, window + contrib[pair_no], corner)
        return lax.fori_loop(0, CAPTURES * LED_MOST, add_block, jnp.zeros_like(spectrum))
    intensity = per_capture(field_real * field_real + field_imag * field_imag)
    misfit = intensity - measured
    gradient = adjoint(misfit) + REG * laplace(spectrum)

    def operator(values):
        return adjoint(forward(values)) + REG * laplace(values)
    spectrum_step = jnp.zeros_like(spectrum)
    cg_residual = -gradient
    heading = cg_residual
    res_norm = jnp.sum(cg_residual * cg_residual)
    for round_no in range(ITERS):
        applied = operator(heading)
        step_len = res_norm / jnp.sum(heading * applied)
        spectrum_step = spectrum_step + step_len * heading
        cg_residual = cg_residual - step_len * applied
        new_norm = jnp.sum(cg_residual * cg_residual)
        heading = cg_residual + new_norm / res_norm * heading
        res_norm = new_norm
    return (spectrum_step, cg_residual)
```

```python
import functools

import jax
import jax.numpy as jnp
import ml_dtypes
import numpy as np
from jax import lax
from jax.experimental import pallas as pl
from jax.experimental.pallas import tpu as pltpu
from jax.sharding import PartitionSpec as P

REG = 0.5
CHUNKS = 4
F32 = jnp.float32
BF16 = jnp.bfloat16
VMEM = pl.BlockSpec(memory_space=pltpu.VMEM)
SMEM = pl.BlockSpec(memory_space=pltpu.SMEM)


def dft_tables(side):
    half = side // 2
    m = np.arange(half)[:, None]
    k = np.arange(half)[None, :]
    out = []
    for q in (0, 1):
        angle = 2 * np.pi * (((2 * m + q) * k) % side) / side
        cos, sin = np.cos(angle) / np.sqrt(side), np.sin(angle) / np.sqrt(side)
        mat = np.block([[cos.T, sin.T], [-sin.T, cos.T]])
        for each in (mat, mat.T):
            high = each.astype(ml_dtypes.bfloat16)
            low = (each - high.astype(np.float64)).astype(ml_dtypes.bfloat16)
            out += [np.ascontiguousarray(high), np.ascontiguousarray(low)]
    return out


def split(x):
    high = x.astype(BF16)
    return high, (x - high.astype(F32)).astype(BF16)


def rmul(x, high, low):
    a, b = split(x)
    return jnp.dot(
        jnp.concatenate([a, b, a], 1),
        jnp.concatenate([high, high, low], 0),
        preferred_element_type=F32,
    )


def lmul(high, low, x):
    a, b = split(x)
    return jnp.dot(
        jnp.concatenate([high, high, low], 1),
        jnp.concatenate([a, b, a], 0),
        preferred_element_type=F32,
    )


def corner(tile, start, side):
    half = side // 2
    row = jnp.minimum(start[0] // 8, (tile[0] - side) // 8 - 1) * 8
    col = jnp.minimum(start[1] // half, tile[1] // half - 3) * half
    return pl.multiple_of(row, 8), pl.multiple_of(col, half), start[0] - row, start[1] - col


def extract(v_ref, part, start, side):
    half = side // 2
    row, col, down, right = corner(v_ref.shape[1:], start, side)
    x = v_ref[part, pl.ds(row, side + 8), pl.ds(col, 3 * half)]
    x = pltpu.roll(x, lax.rem(side + 8 - down, side + 8), 0)[:side]
    back = lax.rem(half - right, half)
    x0, x1, x2 = [pltpu.roll(x[:, i * half : (i + 1) * half], back, 1) for i in range(3)]
    keep = lax.broadcasted_iota(jnp.int32, (side, half), 1) < half - right
    return jnp.where(keep, x0, x1), jnp.where(keep, x1, x2)


def deposit(acc_ref, part, start, x0, x1, side):
    half = side // 2
    row, col, down, right = corner(acc_ref.shape[1:], start, side)
    turn = lax.rem(right, half)
    x0, x1 = pltpu.roll(x0, turn, 1), pltpu.roll(x1, turn, 1)
    keep = lax.broadcasted_iota(jnp.int32, (side, half), 1) >= right
    y = jnp.concatenate(
        [jnp.where(keep, x0, 0.0), jnp.where(keep, x1, x0), jnp.where(keep, 0.0, x1)], 1
    )
    y = jnp.concatenate([y, jnp.zeros((8, 3 * half), F32)], 0)
    y = pltpu.roll(y, down, 0)
    at = (part, pl.ds(row, side + 8), pl.ds(col, 3 * half))
    acc_ref[at] = acc_ref[at] + y


def to_image(v_ref, pupil_ref, tabs, start):
    side = pupil_ref.shape[0]
    half = side // 2
    r0h, r0l, r0th, r0tl, r1h, r1l, r1th, r1tl = tabs
    p0, p1 = pupil_ref[:, :half], pupil_ref[:, half:]
    plus, minus = [], []
    for part in (0, 1):
        x0, x1 = extract(v_ref, part, start, side)
        x0, x1 = x0 * p0, x1 * p1
        plus.append(x0 + x1)
        minus.append(x0 - x1)
    even = rmul(jnp.concatenate(plus, 1), r0h[...], r0l[...])
    odd = rmul(jnp.concatenate(minus, 1), r1h[...], r1l[...])
    re = jnp.concatenate([even[:, :half], odd[:, :half]], 1)
    im = jnp.concatenate([even[:, half:], odd[:, half:]], 1)
    top = jnp.concatenate([re[:half] + re[half:], im[:half] + im[half:]], 0)
    low = jnp.concatenate([re[:half] - re[half:], im[:half] - im[half:]], 0)
    even = lmul(r0th[...], r0tl[...], top)
    odd = lmul(r1th[...], r1tl[...], low)
    return (
        jnp.concatenate([even[:half], odd[:half]], 0),
        jnp.concatenate([even[half:], odd[half:]], 0),
    )


def from_image(re, im, pupil_ref, tabs):
    side = pupil_ref.shape[0]
    half = side // 2
    r0h, r0l, r0th, r0tl, r1h, r1l, r1th, r1tl = tabs
    even = lmul(r0h[...], r0l[...], jnp.concatenate([re[:half], im[:half]], 0))
    odd = lmul(r1h[...], r1l[...], jnp.concatenate([re[half:], im[half:]], 0))
    top, low = even + odd, even - odd
    re = jnp.concatenate([top[:half], low[:half]], 0)
    im = jnp.concatenate([top[half:], low[half:]], 0)
    even = rmul(jnp.concatenate([re[:, :half], im[:, :half]], 1), r0th[...], r0tl[...])
    odd = rmul(jnp.concatenate([re[:, half:], im[:, half:]], 1), r1th[...], r1tl[...])
    p0, p1 = pupil_ref[:, :half], pupil_ref[:, half:]
    left, right = even + odd, even - odd
    return [
        (left[:, :half] * p0, right[:, :half] * p1),
        (left[:, half:] * p0, right[:, half:] * p1),
    ]


def tiles(x):
    rows, cols = x.shape
    x = jnp.sum(x.reshape(rows // 8, 8, cols), 0)
    return sum(x[:, i * 128 : (i + 1) * 128] for i in range(cols // 128))


def total(tile_ref):
    return jnp.sum(jnp.sum(tile_ref[...], 0, keepdims=True), 1, keepdims=True)


def side_columns(left_ref, right_ref, cols_ref):
    size = left_ref.shape[1]
    rows = jnp.concatenate([left_ref[...], right_ref[...], jnp.zeros((4, size), F32)], 0)
    cols_ref[...] = jnp.transpose(rows)


def laplace_rows(v_ref, halo, cols_ref, part, at, count):
    top_ref, bottom_ref = halo[:2]
    rows, cols = v_ref.shape[1:]
    here = v_ref[part, at : at + count, :]
    up = (
        jnp.concatenate([top_ref[part : part + 1, :], v_ref[part, : count - 1, :]], 0)
        if at == 0
        else v_ref[part, at - 1 : at + count - 1, :]
    )
    down = (
        jnp.concatenate([v_ref[part, at + 1 :, :], bottom_ref[part : part + 1, :]], 0)
        if at + count == rows
        else v_ref[part, at + 1 : at + count + 1, :]
    )
    lane = lax.broadcasted_iota(jnp.int32, (count, cols), 1)
    span = slice(at, at + count)
    before = jnp.where(lane == 0, cols_ref[span, part : part + 1], pltpu.roll(here, 1, 1))
    after = jnp.where(
        lane == cols - 1, cols_ref[span, 2 + part : 3 + part], pltpu.roll(here, cols - 1, 1)
    )
    return here, 4.0 * here - (up + down + before + after)


def write_edges(v_ref, edges):
    top_ref, bottom_ref, left_ref, right_ref = edges
    rows, cols = v_ref.shape[1:]
    for part in (0, 1):
        top_ref[part : part + 1, :] = v_ref[part, 0:1, :]
        bottom_ref[part : part + 1, :] = v_ref[part, rows - 1 : rows, :]
        left_ref[part : part + 1, :] = jnp.transpose(v_ref[part, :, :128])[:1]
        right_ref[part : part + 1, :] = jnp.transpose(v_ref[part, :, cols - 128 :])[127:128]


def store_image(chunk_refs, i, image):
    rows = chunk_refs[0].shape[1]
    for j, ref in enumerate(chunk_refs):
        ref[i] = image[j * rows : (j + 1) * rows]


def load_image(chunk_refs, i):
    return jnp.concatenate([ref[i] for ref in chunk_refs], 0)


def reversed_bits(i, count):
    return sum(((i >> b) & 1) << (count - 1 - b) for b in range(count))


def fields_kernel(first, base, led_ref, v_ref, pupil_ref, measured_ref, swap_ref, *refs):
    tabs, rest = refs[:8], refs[8:]
    chunk_refs, field_ref, slot_ref = rest[:CHUNKS], rest[CHUNKS], rest[CHUNKS + 1]
    across = lax.axis_size("tx")
    bits = across.bit_length() - 1
    slots = (led_ref.shape[1] - 1) // 3
    row_start = lax.axis_index("ty") * across
    column = lax.axis_index("tx")
    for i in range(across):
        capture = row_start + jnp.bitwise_xor(column, reversed_bits(i, bits))
        row = col = live = jnp.int32(0)
        for t in range(slots):
            hit = jnp.where(
                (led_ref[capture, 1 + t] == column) & (t < led_ref[capture, 0]), 1, 0
            )
            row += hit * led_ref[capture, 1 + slots + 2 * t]
            col += hit * led_ref[capture, 2 + slots + 2 * t]
            live += hit
        slot_ref[i, 0] = row
        slot_ref[i, 1] = col
        slot_ref[i, 2] = live

    def body(i, carry):
        at = base + i

        @pl.when(slot_ref[at, 2] > 0)
        def _():
            re, im = to_image(v_ref, pupil_ref, tabs, (slot_ref[at, 0], slot_ref[at, 1]))
            field_ref[i, 0] = 2.0 * re
            field_ref[i, 1] = 2.0 * im
            store_image(chunk_refs, i, re * re + im * im)

        @pl.when(slot_ref[at, 2] == 0)
        def _():
            field_ref[i] = jnp.zeros(field_ref.shape[1:], F32)
            store_image(chunk_refs, i, jnp.zeros(field_ref.shape[2:], F32))

        return carry

    lax.fori_loop(0, field_ref.shape[0], body, 0)
    if first:
        highest = lax.Precision.HIGHEST
        swap = swap_ref[...]
        image = jnp.dot(swap, measured_ref[0], precision=highest, preferred_element_type=F32)
        image = lax.dot_general(
            image, swap, (((1,), (1,)), ((), ())), precision=highest, preferred_element_type=F32
        )
        store_image(chunk_refs, 0, load_image(chunk_refs, 0) - image)


def linear_images(base, slot_ref, v_ref, pupil_ref, tabs, field_ref, chunk_refs):
    def body(i, carry):
        at = base + i

        @pl.when(slot_ref[at, 2] > 0)
        def _():
            re, im = to_image(v_ref, pupil_ref, tabs, (slot_ref[at, 0], slot_ref[at, 1]))
            store_image(chunk_refs, i, field_ref[i, 0] * re + field_ref[i, 1] * im)

        @pl.when(slot_ref[at, 2] == 0)
        def _():
            store_image(chunk_refs, i, jnp.zeros(field_ref.shape[2:], F32))

        return carry

    lax.fori_loop(0, field_ref.shape[0], body, 0)


def deposit_images(base, slot_ref, image_at, field_ref, pupil_ref, tabs, acc_ref):
    side = pupil_ref.shape[0]

    def body(i, carry):
        at = base + i

        @pl.when(slot_ref[at, 2] > 0)
        def _():
            image = image_at(i)
            parts = from_image(field_ref[i, 0] * image, field_ref[i, 1] * image, pupil_ref, tabs)
            start = (slot_ref[at, 0], slot_ref[at, 1])
            for part in (0, 1):
                deposit(acc_ref, part, start, *parts[part], side)

        return carry

    lax.fori_loop(0, field_ref.shape[0], body, 0)


def linear_kernel(base, slot_ref, v_ref, pupil_ref, field_ref, *refs):
    tabs, chunk_refs = refs[:8], refs[8:]
    linear_images(base, slot_ref, v_ref, pupil_ref, tabs, field_ref, chunk_refs)


def adjoint_kernel(base, slot_ref, pupil_ref, field_ref, *refs):
    tabs, chunk_refs, acc_ref = refs[:8], refs[8 : 8 + CHUNKS], refs[8 + CHUNKS]
    acc_ref[...] = jnp.zeros(acc_ref.shape, F32)
    deposit_images(
        base, slot_ref, lambda i: load_image(chunk_refs, i), field_ref, pupil_ref, tabs, acc_ref
    )


def turn_kernel(base, sign, slot_ref, pupil_ref, field_ref, part_ref, v_ref, *refs):
    halo, refs = refs[:4], refs[4:]
    tabs, refs = refs[:8], refs[8:]
    in_refs, refs = refs[:CHUNKS], refs[CHUNKS:]
    out_ref, norm_ref, refs = refs[0], refs[1], refs[2:]
    edges, refs = refs[:4], refs[4:]
    chunk_refs, (cols_ref,) = refs[:CHUNKS], refs[CHUNKS:]
    out_ref[...] = part_ref[...]
    deposit_images(
        base, slot_ref, lambda i: load_image(in_refs, i), field_ref, pupil_ref, tabs, out_ref
    )
    side_columns(halo[2], halo[3], cols_ref)
    count = 64
    norm = jnp.zeros((8, 128), F32)
    for part in (0, 1):
        for at in range(0, v_ref.shape[1], count):
            _, bent = laplace_rows(v_ref, halo, cols_ref, part, at, count)
            value = sign * (out_ref[part, at : at + count, :] + REG * bent)
            out_ref[part, at : at + count, :] = value
            norm += tiles(value * value)
    norm_ref[...] = norm
    write_edges(out_ref, edges)
    linear_images(base, slot_ref, out_ref, pupil_ref, tabs, field_ref, chunk_refs)


def bend_kernel(v_ref, *refs):
    halo, (out_ref, cols_ref) = refs[:4], refs[4:]
    side_columns(halo[2], halo[3], cols_ref)
    count = 64
    found = jnp.zeros((8, 128), F32)
    for part in (0, 1):
        for at in range(0, v_ref.shape[1], count):
            here, bent = laplace_rows(v_ref, halo, cols_ref, part, at, count)
            found += tiles(here * bent)
    out_ref[...] = found


def step_size(sums_ref, curve_ref):
    return total(sums_ref.at[0]) / (total(curve_ref) + REG * total(sums_ref.at[1]))


def residual_kernel(r0_ref, q0_ref, sums_ref, curve_ref, *refs):
    halo_r, halo_q, refs = refs[:4], refs[4:8], refs[8:]
    r1_ref, found_ref = refs[:2]
    halo_1 = refs[2:6]
    cols_ref, cols0_ref = refs[6:]
    alpha = step_size(sums_ref, curve_ref)
    for a, b, c in zip(halo_r, halo_q, halo_1):
        c[...] = a[...] - alpha * b[...]
    side_columns(halo_1[2], halo_1[3], cols_ref)
    side_columns(halo_r[2], halo_r[3], cols0_ref)
    count = 64
    sums = [jnp.zeros((8, 128), F32) for _ in range(3)]
    for part in (0, 1):
        for at in range(0, r0_ref.shape[1], count):
            span = slice(at, at + count)
            r1_ref[part, span, :] = r0_ref[part, span, :] - alpha * q0_ref[part, span, :]
        for at in range(0, r0_ref.shape[1], count):
            here, bent = laplace_rows(r1_ref, halo_1, cols_ref, part, at, count)
            _, bent0 = laplace_rows(r0_ref, halo_r, cols0_ref, part, at, count)
            sums[0] += tiles(here * here)
            sums[1] += tiles(here * bent)
            sums[2] += tiles(here * bent0)
    for i in range(3):
        found_ref[i] = sums[i]


def last_adjoint_kernel(base, slot_ref, pupil_ref, field_ref, *refs):
    tabs, refs = refs[:8], refs[8:]
    first_refs, second_refs = refs[:CHUNKS], refs[CHUNKS : 2 * CHUNKS]
    refs = refs[2 * CHUNKS :]
    sums_ref, curve_ref, later_ref = refs[:3]
    if base:
        part_ref, acc_ref = refs[3:]
        acc_ref[...] = part_ref[...]
    else:
        acc_ref = refs[3]
        acc_ref[...] = jnp.zeros(acc_ref.shape, F32)
    alpha = step_size(sums_ref, curve_ref)
    beta = total(later_ref.at[0]) / total(sums_ref.at[0])

    def image_at(i):
        return (1.0 + beta) * load_image(first_refs, i) - alpha * load_image(second_refs, i)

    deposit_images(base, slot_ref, image_at, field_ref, pupil_ref, tabs, acc_ref)


def images_norm_kernel(sums_ref, curve_ref, later_ref, *refs):
    firsts, seconds, out_ref = refs[: 2 * CHUNKS], refs[2 * CHUNKS : 4 * CHUNKS], refs[4 * CHUNKS]
    alpha = step_size(sums_ref, curve_ref)
    beta = total(later_ref.at[0]) / total(sums_ref.at[0])

    def body(i, acc):
        for a, b in zip(firsts, seconds):
            w = (1.0 + beta) * a[i] - alpha * b[i]
            acc += tiles(w * w)
        return acc

    out_ref[...] = lax.fori_loop(0, firsts[0].shape[0], body, jnp.zeros((8, 128), F32))


def first_norm_kernel(*refs):
    firsts, out_ref = refs[:-1], refs[-1]

    def body(i, acc):
        for a in firsts:
            acc += tiles(a[i] * a[i])
        return acc

    out_ref[...] = lax.fori_loop(0, firsts[0].shape[0], body, jnp.zeros((8, 128), F32))


def finish_kernel(r0_ref, r1_ref, acc_ref, sums_ref, curve_ref, later_ref, last_ref, *refs):
    halo_r, halo_1, refs = refs[:4], refs[4:8], refs[8:]
    step_ref, res_ref, h_ref, cols_ref = refs[:4]
    halo_h = refs[4:8]
    alpha = step_size(sums_ref, curve_ref)
    norm0, norm1 = total(sums_ref.at[0]), total(later_ref.at[0])
    beta = norm1 / norm0
    bend = (
        total(later_ref.at[1])
        + 2.0 * beta * total(later_ref.at[2])
        + beta * beta * total(sums_ref.at[1])
    )
    alpha1 = norm1 / (total(last_ref) + REG * bend)
    for a, b, c in zip(halo_r, halo_1, halo_h):
        c[...] = b[...] + beta * a[...]
    side_columns(halo_h[2], halo_h[3], cols_ref)
    count = 64
    for part in (0, 1):
        for at in range(0, r0_ref.shape[1], count):
            span = slice(at, at + count)
            h_ref[part, span, :] = r1_ref[part, span, :] + beta * r0_ref[part, span, :]
        for at in range(0, r0_ref.shape[1], count):
            span = slice(at, at + count)
            here, bent = laplace_rows(h_ref, halo_h, cols_ref, part, at, count)
            step_ref[part, span, :] = alpha * r0_ref[part, span, :] + alpha1 * here
            res_ref[part, span, :] = r1_ref[part, span, :] - alpha1 * (
                acc_ref[part, span, :] + REG * bent
            )


def call(kernel, name, out, operands, smem=0, scratch=(), flops=0, smem_out=False):
    out_specs = [VMEM] * len(out)
    if smem_out:
        out_specs[-1] = SMEM
    cost = pl.CostEstimate(
        flops=flops,
        bytes_accessed=sum(x.size * x.dtype.itemsize for x in list(operands) + list(out)),
        transcendentals=0,
    )
    return list(pl.pallas_call(
        kernel,
        out_shape=out,
        in_specs=[SMEM] * smem + [VMEM] * (len(operands) - smem),
        out_specs=out_specs,
        scratch_shapes=list(scratch),
        compiler_params=pltpu.CompilerParams(vmem_limit_bytes=48 << 20),
        cost_estimate=cost,
        name=name,
    )(*operands))


def shift(x, axis, by):
    size = lax.axis_size(axis)
    pairs = [(i, i + by) for i in range(size) if 0 <= i + by < size]
    return lax.ppermute(x, axis, pairs)


def exchange(x, axis, bit):
    return lax.ppermute(x, axis, [(i, i ^ bit) for i in range(lax.axis_size(axis))])


def halo_of(edges):
    top, bottom, left, right = edges
    return [
        shift(bottom, "ty", 1),
        shift(top, "ty", -1),
        shift(right, "tx", 1),
        shift(left, "tx", -1),
    ]


def all_bits(axis):
    return [1 << b for b in range(lax.axis_size(axis).bit_length() - 1)]


def sum_over(x, axes):
    for axis in axes:
        for bit in all_bits(axis):
            x = x + exchange(x, axis, bit)
    return x


def reduce_images(near, far, order):
    bits = all_bits("tx")
    shape = near.shape[1:]
    if order[0] == bits[0]:
        kept, got = near, exchange(far, "tx", bits[0])
        x = (kept + got).reshape((1,) + (2,) * (len(bits) - 1) + shape)
        done = [bits[0]]
    else:
        x = jnp.stack([near, far]).reshape((2,) * len(bits) + shape)
        done = []
    for bit in order[len(done) : -1]:
        axis = bits.index(bit)
        low, high = jnp.split(x, 2, axis)
        x = low + exchange(high, "tx", bit)
        done.append(bit)
    axis = bits.index(order[-1])
    x = x + jnp.flip(exchange(x, "tx", order[-1]), axis)
    for bit in done[::-1]:
        if bit == bits[0] and done[0] == bit:
            near = x.reshape((-1,) + shape)
            return near, exchange(near, "tx", bit)
        x = jnp.concatenate([x, exchange(x, "tx", bit)], bits.index(bit))
    x = x.reshape((2, -1) + shape)
    return x[0], x[1]


def on_device(spectrum, measured, pupil_mask, led_count, led_owner, led_offset):
    side = pupil_mask.shape[0]
    across = lax.axis_size("tx")
    part = across // 2
    captures, slots = led_owner.shape
    pupil = pupil_mask.astype(F32)
    led = jnp.concatenate(
        [led_count[:, None], led_owner, led_offset.reshape(captures, 2 * slots)], axis=1
    )
    tabs = [jnp.asarray(x) for x in dft_tables(side)]
    swap = np.zeros((side, side), np.float32)
    swap[np.arange(side), np.r_[0:side:2, 1:side:2]] = 1.0
    swap = jnp.asarray(swap)
    bits = all_bits("tx")
    orders = [bits] * (CHUNKS - 1) + [bits[1:] + bits[:1]]

    field_t = jax.ShapeDtypeStruct((part, 2, side, side), F32)
    chunk_t = jax.ShapeDtypeStruct((part, side // CHUNKS, side), F32)
    slot_t = jax.ShapeDtypeStruct((across, 4), jnp.int32)
    tile_t = jax.ShapeDtypeStruct(spectrum.shape, F32)
    sum_t = jax.ShapeDtypeStruct((8, 128), F32)
    row_t = jax.ShapeDtypeStruct((2, spectrum.shape[2]), F32)
    col_t = jax.ShapeDtypeStruct((2, spectrum.shape[1]), F32)
    edge_t = [row_t, row_t, col_t, col_t]
    cols_s = pltpu.VMEM((spectrum.shape[1], 8), F32)
    flops = part * 8 * 3 * side**3 * 2

    def reduced(near, far):
        done = [reduce_images(a, b, o) for a, b, o in zip(near, far, orders)]
        return [d[0] for d in done], [d[1] for d in done]

    def fields(first):
        base = 0 if first else part
        out = call(
            functools.partial(fields_kernel, first, base),
            "fields_%d" % base,
            [chunk_t] * CHUNKS + [field_t, slot_t],
            [led, spectrum, pupil, measured, swap] + tabs,
            smem=1,
            flops=flops,
            smem_out=True,
        )
        return out[:CHUNKS], out[CHUNKS], out[CHUNKS + 1]

    def adjoint(near):
        return call(
            functools.partial(adjoint_kernel, 0),
            "adjoint",
            [tile_t],
            [slot, pupil, field_near] + tabs + near,
            smem=1,
            flops=flops,
        )[0]

    def turn(sign, acc, far, values, halo):
        out = call(
            functools.partial(turn_kernel, part, sign),
            "turn",
            [tile_t, sum_t] + edge_t + [chunk_t] * CHUNKS,
            [slot, pupil, field_far, acc, values] + halo + tabs + far,
            smem=1,
            scratch=[cols_s],
            flops=2 * flops,
        )
        return out[0], out[1], out[2:6], out[6:]

    def linear(values):
        return call(
            functools.partial(linear_kernel, 0),
            "linear",
            [chunk_t] * CHUNKS,
            [slot, values, pupil, field_near] + tabs,
            smem=1,
            flops=flops,
        )

    far, field_far, slot = fields(False)
    near, field_near, _ = fields(True)
    halo_s = halo_of(
        [spectrum[:, 0, :], spectrum[:, -1, :], spectrum[:, :, 0], spectrum[:, :, -1]]
    )
    near, far = reduced(near, far)

    r0, r0_norm, edges, far = turn(-1.0, adjoint(near), far, spectrum, halo_s)
    near = linear(r0)
    halo_r = halo_of(edges)
    r0_bend = call(bend_kernel, "bend", [sum_t], [r0] + halo_r, scratch=[cols_s])[0]
    sums = sum_over(jnp.stack([r0_norm, r0_bend]), ("ty", "tx"))
    near0, far0 = reduced(near, far)

    curve = call(first_norm_kernel, "first_norm", [sum_t], near0 + far0)[0]
    curve = sum_over(curve, ("ty",))
    q0, _, edges, far = turn(1.0, adjoint(near0), far0, r0, halo_r)
    near = linear(q0)
    halo_q = halo_of(edges)
    out = call(
        residual_kernel,
        "residual",
        [tile_t, jax.ShapeDtypeStruct((3, 8, 128), F32)] + edge_t,
        [r0, q0, sums, curve] + halo_r + halo_q,
        scratch=[cols_s, cols_s],
    )
    r1, later, halo_1 = out[0], out[1], out[2:6]
    later = sum_over(later, ("ty", "tx"))
    near1, far1 = reduced(near, far)

    last = call(
        images_norm_kernel,
        "images_norm",
        [sum_t],
        [sums, curve, later] + near0 + far0 + near1 + far1,
    )[0]
    last = sum_over(last, ("ty",))
    acc = call(
        functools.partial(last_adjoint_kernel, 0),
        "last_adjoint_near",
        [tile_t],
        [slot, pupil, field_near] + tabs + near0 + near1 + [sums, curve, later],
        smem=1,
        flops=flops,
    )[0]
    acc = call(
        functools.partial(last_adjoint_kernel, part),
        "last_adjoint_far",
        [tile_t],
        [slot, pupil, field_far] + tabs + far0 + far1 + [sums, curve, later, acc],
        smem=1,
        flops=flops,
    )[0]
    return tuple(
        call(
            finish_kernel,
            "finish",
            [tile_t, tile_t],
            [r0, r1, acc, sums, curve, later, last] + halo_r + halo_1,
            scratch=[pltpu.VMEM(tile_t.shape, F32), cols_s]
            + [pltpu.VMEM(t.shape, F32) for t in edge_t],
        )
    )


def solution(mesh):
    placed = (P(None, "ty", "tx"), P(("ty", "tx"), None, None), P(), P(), P(), P())
    return jax.shard_map(
        on_device,
        mesh=mesh,
        in_specs=placed,
        out_specs=(P(None, "ty", "tx"), P(None, "ty", "tx")),
        check_vma=False,
    )
```

```python
import functools

import jax
import jax.numpy as jnp
import ml_dtypes
import numpy as np
from jax import lax
from jax.experimental import pallas as pl
from jax.experimental.pallas import tpu as pltpu
from jax.sharding import PartitionSpec as P

REG = 0.5
ROWS = 64
F32 = jnp.float32
BF16 = jnp.bfloat16
VMEM = pl.BlockSpec(memory_space=pltpu.VMEM)
SMEM = pl.BlockSpec(memory_space=pltpu.SMEM)


def dft_tables(side):
    half = side // 2
    m = np.arange(half)[:, None]
    k = np.arange(half)[None, :]
    out = []
    for q in (0, 1):
        angle = 2 * np.pi * (((2 * m + q) * k) % side) / side
        cos, sin = np.cos(angle) / np.sqrt(side), np.sin(angle) / np.sqrt(side)
        mat = np.block([[cos.T, sin.T], [-sin.T, cos.T]])
        for each in (mat, mat.T):
            high = each.astype(ml_dtypes.bfloat16)
            low = (each - high.astype(np.float64)).astype(ml_dtypes.bfloat16)
            out += [high, low]
    return np.stack(out)


def split(x):
    high = x.astype(BF16)
    return high, (x - high.astype(F32)).astype(BF16)


def rmul(x, tab_ref, at):
    a, b = split(x)
    high, low = tab_ref[at], tab_ref[at + 1]
    return jnp.dot(
        jnp.concatenate([a, b, a], 1),
        jnp.concatenate([high, high, low], 0),
        preferred_element_type=F32,
    )


def lmul(tab_ref, at, x):
    a, b = split(x)
    high, low = tab_ref[at], tab_ref[at + 1]
    return jnp.dot(
        jnp.concatenate([high, high, low], 1),
        jnp.concatenate([a, b, a], 0),
        preferred_element_type=F32,
    )


def masks(start, side):
    rows = lax.broadcasted_iota(jnp.int32, (side, side // 2), 0) >= start[0]
    lane = lax.broadcasted_iota(jnp.int32, (side, side // 2), 1)
    return rows, [lane + j * (side // 2) >= start[1] for j in (0, 1)]


def extract(v_ref, part, start, side):
    half = side // 2
    rows, cols = masks(start, side)
    out = []
    for j in (0, 1):
        near, far = slice(j * half, (j + 1) * half), slice(side + j * half, side + (j + 1) * half)
        top = jnp.where(cols[j], v_ref[part, :side, near], v_ref[part, :side, far])
        low = jnp.where(cols[j], v_ref[part, side:, near], v_ref[part, side:, far])
        out.append(jnp.where(rows, top, low))
    return out


def deposit(acc_ref, part, start, halves, side):
    half = side // 2
    rows, cols = masks(start, side)
    for j, x in enumerate(halves):
        top, low = jnp.where(rows, x, 0.0), jnp.where(rows, 0.0, x)
        for at, value in ((slice(0, side), top), (slice(side, 2 * side), low)):
            near = (part, at, slice(j * half, (j + 1) * half))
            far = (part, at, slice(side + j * half, side + (j + 1) * half))
            acc_ref[near] = acc_ref[near] + jnp.where(cols[j], value, 0.0)
            acc_ref[far] = acc_ref[far] + jnp.where(cols[j], 0.0, value)


def to_image(v_ref, pupil, tab_ref, start):
    side = pupil.shape[0]
    half = side // 2
    plus, minus = [], []
    for part in (0, 1):
        x0, x1 = extract(v_ref, part, start, side)
        x0, x1 = x0 * pupil[:, :half], x1 * pupil[:, half:]
        plus.append(x0 + x1)
        minus.append(x0 - x1)
    even = rmul(jnp.concatenate(plus, 1), tab_ref, 0)
    odd = rmul(jnp.concatenate(minus, 1), tab_ref, 4)
    re = jnp.concatenate([even[:, :half], odd[:, :half]], 1)
    im = jnp.concatenate([even[:, half:], odd[:, half:]], 1)
    top = jnp.concatenate([re[:half] + re[half:], im[:half] + im[half:]], 0)
    low = jnp.concatenate([re[:half] - re[half:], im[:half] - im[half:]], 0)
    even = lmul(tab_ref, 2, top)
    odd = lmul(tab_ref, 6, low)
    return (
        jnp.concatenate([even[:half], odd[:half]], 0),
        jnp.concatenate([even[half:], odd[half:]], 0),
    )


def from_image(re, im, pupil, tab_ref):
    side = pupil.shape[0]
    half = side // 2
    even = lmul(tab_ref, 0, jnp.concatenate([re[:half], im[:half]], 0))
    odd = lmul(tab_ref, 4, jnp.concatenate([re[half:], im[half:]], 0))
    top, low = even + odd, even - odd
    re = jnp.concatenate([top[:half], low[:half]], 0)
    im = jnp.concatenate([top[half:], low[half:]], 0)
    even = rmul(jnp.concatenate([re[:, :half], im[:, :half]], 1), tab_ref, 2)
    odd = rmul(jnp.concatenate([re[:, half:], im[:, half:]], 1), tab_ref, 6)
    p0, p1 = pupil[:, :half], pupil[:, half:]
    left, right = even + odd, even - odd
    return [
        (left[:, :half] * p0, right[:, :half] * p1),
        (left[:, half:] * p0, right[:, half:] * p1),
    ]


def tiles(x):
    rows, cols = x.shape
    x = jnp.sum(x.reshape(rows // 8, 8, cols), 0)
    return sum(x[:, i * 128 : (i + 1) * 128] for i in range(cols // 128))


def total(tile):
    return jnp.sum(jnp.sum(tile, 0, keepdims=True), 1, keepdims=True)


def side_columns(left_ref, right_ref, cols_ref):
    size = left_ref.shape[1]
    rows = jnp.concatenate([left_ref[...], right_ref[...], jnp.zeros((4, size), F32)], 0)
    cols_ref[...] = jnp.transpose(rows)


def laplace_rows(v_ref, halo, cols_ref, part, at, count):
    top_ref, bottom_ref = halo[:2]
    rows, cols = v_ref.shape[1:]
    here = v_ref[part, at : at + count, :]
    up = (
        jnp.concatenate([top_ref[part : part + 1, :], v_ref[part, : count - 1, :]], 0)
        if at == 0
        else v_ref[part, at - 1 : at + count - 1, :]
    )
    down = (
        jnp.concatenate([v_ref[part, at + 1 :, :], bottom_ref[part : part + 1, :]], 0)
        if at + count == rows
        else v_ref[part, at + 1 : at + count + 1, :]
    )
    lane = lax.broadcasted_iota(jnp.int32, (count, cols), 1)
    span = slice(at, at + count)
    before = jnp.where(lane == 0, cols_ref[span, part : part + 1], pltpu.roll(here, 1, 1))
    after = jnp.where(
        lane == cols - 1, cols_ref[span, 2 + part : 3 + part], pltpu.roll(here, cols - 1, 1)
    )
    return here, 4.0 * here - (up + down + before + after)


def write_edges(v_ref, edges):
    top_ref, bottom_ref, left_ref, right_ref = edges
    rows, cols = v_ref.shape[1:]
    for part in (0, 1):
        top_ref[part : part + 1, :] = v_ref[part, 0:1, :]
        bottom_ref[part : part + 1, :] = v_ref[part, rows - 1 : rows, :]
        left_ref[part : part + 1, :] = jnp.transpose(v_ref[part, :, :128])[:1]
        right_ref[part : part + 1, :] = jnp.transpose(v_ref[part, :, cols - 128 :])[127:128]


def each(count, always, slot_ref, base, work):
    def body(i, carry):
        if always:
            work(i)
        else:
            pl.when(slot_ref[base + i, 2] > 0)(lambda: work(i))
        return carry

    lax.fori_loop(0, count, body, 0, unroll=2 if always else 1)


def unpack(refs, *counts):
    out = []
    for count in counts:
        out.append(refs[0] if count is None else refs[:count])
        refs = refs[1 if count is None else count :]
    assert not refs
    return out


def find_slots(count_ref, owner_ref, offset_ref, slot_ref):
    slots = owner_ref.shape[0]
    across = lax.axis_size("tx")
    row_start = lax.axis_index("ty") * across
    column = lax.axis_index("tx")
    order = positions(across)
    for i in range(across):
        capture = row_start + jnp.bitwise_xor(column, order[i])
        row = col = live = jnp.int32(0)
        for t in range(slots):
            hit = jnp.where((owner_ref[t, capture] == column) & (t < count_ref[capture]), 1, 0)
            row += hit * offset_ref[t, 0, capture]
            col += hit * offset_ref[t, 1, capture]
            live += hit
        slot_ref[i, 0] = row
        slot_ref[i, 1] = col
        slot_ref[i, 2] = live


def fields_kernel(near, *refs):
    if near:
        (slot_ref, slots_ref, v_ref, mask_ref, tab_ref, measured_ref, swap_ref), images, (
            field_ref,
            pupil_ref,
        ) = unpack(refs, 7, 5, 2)
        slots = slots_ref.shape[0]
        across = slot_ref.shape[0]
    else:
        given, images, (field_ref, pupil_ref), edges, slot_ref, kept, sems = unpack(
            refs, 6, 3, 2, 4, None, 6, None
        )
        copies = [pltpu.make_async_copy(a, b, sems.at[i]) for i, (a, b) in enumerate(zip(given, kept))]
        for copy in copies:
            copy.start()
        for copy in copies[:3]:
            copy.wait()
        count_ref, owner_ref, offset_ref, v_ref, mask_ref, tab_ref = kept
        slots, across = owner_ref.shape[0], lax.axis_size("tx")
        find_slots(count_ref, owner_ref, offset_ref, slot_ref)
        for copy in copies[3:]:
            copy.wait()
    part = across // 2
    base = 0 if near else part
    upper, lowers = image_refs(near, images)
    rows = upper.shape[1]
    count = part // 2
    always = slots >= across
    if not always:
        clear([upper, field_ref, pupil_ref] + [ref.at[:count] for ref in lowers])
    mask = mask_ref[...].astype(F32)
    for z in (0, 1):

        def work(i):
            at = z * count + i
            start = (slot_ref[base + at, 0], slot_ref[base + at, 1])
            side = mask.shape[0]
            pupil = pltpu.roll(mask, lax.rem(start[0], side), 0)
            pupil_ref[at] = pltpu.roll(pupil, lax.rem(start[1], side), 1)
            pupil = pupil_ref[at]
            live = slot_ref[base + at, 2].astype(F32)
            re, im = to_image(v_ref, pupil, tab_ref, start)
            re, im = re * live, im * live
            field_ref[at, 0] = 2.0 * re
            field_ref[at, 1] = 2.0 * im
            image = re * re + im * im
            upper[at] = image[:rows]
            lowers[z][i] = image[rows:]

        each(count, always, slot_ref, base + z * count, work)
    if near:
        highest = lax.Precision.HIGHEST
        swap = swap_ref[...]
        image = jnp.dot(swap, measured_ref[0], precision=highest, preferred_element_type=F32)
        image = lax.dot_general(
            image, swap, (((1,), (1,)), ((), ())), precision=highest, preferred_element_type=F32
        )
        upper[0] = upper[0] - image[:rows]
        lowers[0][0] = lowers[0][0] - image[rows:]
    else:
        write_edges(v_ref, edges)


def deposit_images(slots, y, z, slot_ref, image_at, field_ref, pupil_ref, tab_ref, acc_ref):
    part, _, side, _ = field_ref.shape
    count = part // 2
    base = y * part + z * count

    def work(i):
        image = image_at(z * count + i, y * count + i)
        at = z * count + i
        parts = from_image(
            field_ref[at, 0] * image, field_ref[at, 1] * image, pupil_ref[at], tab_ref
        )
        start = (slot_ref[base + i, 0], slot_ref[base + i, 1])
        for part in (0, 1):
            deposit(acc_ref, part, start, parts[part], side)

    each(count, slots >= 2 * part, slot_ref, base, work)


def image_refs(near, refs):
    if near:
        came, upper, lowers = unpack(refs, 2, None, 2)
        count = came[0].shape[0]
        for a, b in zip(came, lowers):
            b[count:] = a[...]
    else:
        upper, lowers = unpack(refs, None, 2)
    return upper, lowers


def clear(refs):
    for ref in refs:
        ref[...] = jnp.zeros(ref.shape, F32)


def linear_kernel(slots, near, slot_ref, v_ref, tab_ref, pupil_ref, field_ref, *refs):
    upper, lowers = image_refs(near, refs[-5:] if near else refs[-3:])
    part = field_ref.shape[0]
    count = part // 2
    base = 0 if near else part
    always = slots >= 2 * part
    if not always:
        clear([upper] + [ref.at[:count] for ref in lowers])
    for z in (0, 1):

        def work(i):
            at = z * count + i
            start = (slot_ref[base + at, 0], slot_ref[base + at, 1])
            re, im = to_image(v_ref, pupil_ref[at], tab_ref, start)
            image = field_ref[at, 0] * re + field_ref[at, 1] * im
            upper[at] = image[: upper.shape[1]]
            lowers[z][i] = image[upper.shape[1] :]

        each(count, always, slot_ref, base + z * count, work)


def one_image(first_ref, second_ref, side):
    rows = side - second_ref.shape[1]
    return lambda a, b: jnp.concatenate([first_ref[a, :rows, :], second_ref[b]], 0)


def adjoint_kernel(slots, slot_ref, start_ref, pupil_ref, field_ref, tab_ref, *refs):
    first_ref, second_ref, acc_ref = refs
    acc_ref[...] = start_ref[...]
    image = one_image(first_ref, second_ref, field_ref.shape[2])
    deposit_images(slots, 0, 0, slot_ref, image, field_ref, pupil_ref, tab_ref, acc_ref)


def turn_kernel(slots, sign, slot_ref, part_ref, tab_ref, *refs):
    pupils, fields, firsts, seconds, refs = refs[:2], refs[2:4], refs[4:6], refs[6:8], refs[8:]
    (out_ref, sum_ref), edges = unpack(refs, 2, 4)
    out_ref[...] = part_ref[...]
    for y, z in ((0, 1), (1, 0), (1, 1)):
        image = one_image(firsts[y], seconds[z], fields[y].shape[2])
        deposit_images(slots, y, z, slot_ref, image, fields[y], pupils[y], tab_ref, out_ref)
    found = jnp.zeros((8, 128), F32)
    if sign < 0:
        for part in (0, 1):
            for at in range(0, out_ref.shape[1], ROWS):
                value = -out_ref[part, at : at + ROWS, :]
                out_ref[part, at : at + ROWS, :] = value
                found += tiles(value * value)
    sum_ref[...] = found
    write_edges(out_ref, edges)


def bend_kernel(v_ref, *refs):
    halo, refs = refs[:4], refs[4:]
    norm_ref, refs = (refs[0], refs[1:]) if len(refs) == 4 else (None, refs)
    bent_ref, sums_ref, cols_ref = refs
    side_columns(halo[2], halo[3], cols_ref)
    found = jnp.zeros((8, 128), F32)
    for part in (0, 1):
        for at in range(0, v_ref.shape[1], ROWS):
            here, bent = laplace_rows(v_ref, halo, cols_ref, part, at, ROWS)
            bent = REG * bent
            bent_ref[part, at : at + ROWS, :] = bent
            found += tiles(here * bent)
    sums_ref[:, 128:] = found
    sums_ref[:, :128] = found if norm_ref is None else norm_ref[...]


def step_size(sums_ref):
    return total(sums_ref[:, :128]) / total(sums_ref[:, 128:])


def residual_kernel(r0_ref, q0_ref, sums_ref, *refs):
    halo_r, halo_q, (r1_ref, bent_ref, found_ref), halo, cols_ref = unpack(refs, 4, 4, 3, 4, None)
    alpha = step_size(sums_ref)
    for a, b, c in zip(halo_r, halo_q, halo):
        c[...] = a[...] - alpha * b[...]
    side_columns(halo[2], halo[3], cols_ref)
    sums = [jnp.zeros((8, 128), F32) for _ in range(2)]
    for part in (0, 1):
        for at in range(0, r0_ref.shape[1], ROWS):
            span = slice(at, at + ROWS)
            r1_ref[part, span, :] = r0_ref[part, span, :] - alpha * q0_ref[part, span, :]
        for at in range(0, r0_ref.shape[1], ROWS):
            span = slice(at, at + ROWS)
            here, bent = laplace_rows(r1_ref, halo, cols_ref, part, at, ROWS)
            bent = REG * bent
            bent_ref[part, span, :] = bent
            sums[0] += tiles(here * here)
            sums[1] += tiles(here * bent)
    found_ref[:, :128] = sums[0]
    found_ref[:, 128:] = sums[1]


def last_kernel(slots, near, slot_ref, start_ref, tab_ref, sums_ref, *refs):
    pupils, fields, w0, wq, acc_ref = unpack(refs, 2, 2, 4, 4, None)
    rows = fields[0].shape[2] - w0[2].shape[1]
    acc_ref[...] = start_ref[...]
    alpha = step_size(sums_ref)
    for y, z in ((0, 0),) if near else ((0, 1), (1, 0), (1, 1)):

        def image(a, b, first=(w0[y], wq[y]), second=(w0[2 + z], wq[2 + z])):
            upper = first[0][a, :rows, :] - alpha * first[1][a, :rows, :]
            return jnp.concatenate([upper, second[0][b] - alpha * second[1][b]], 0)

        deposit_images(slots, y, z, slot_ref, image, fields[y], pupils[y], tab_ref, acc_ref)


def norm_kernel(rows, count, *refs):
    sums_ref, refs = (refs[0], refs[1:]) if count == 2 else (None, refs)
    w0, refs = refs[:4], refs[4:]
    wq, out_ref = (refs[:4], refs[4]) if count == 2 else (None, refs[0])
    alpha = step_size(sums_ref) if count == 2 else None

    def body(i, acc):
        for j in range(4):
            w = w0[j][i, :rows, :] if j < 2 else w0[j][i]
            if wq:
                w = w - alpha * (wq[j][i, :rows, :] if j < 2 else wq[j][i])
            acc += tiles(w * w)
        return acc

    part = w0[0].shape[0]
    squares = lax.fori_loop(0, part, body, jnp.zeros((8, 128), F32))
    came = jnp.zeros((8, 256), F32)
    for ref in (wq or w0)[:2]:
        for i in range(part):
            came += ref[i, rows:, :]
    out_ref[:, :128] = came[:, :128]
    out_ref[:, 128:] = came[:, 128:] + squares


def finish_kernel(r0_ref, r1_ref, q0_ref, acc_ref, sums_ref, later_ref, *refs):
    step_ref, res_ref = refs
    alpha = step_size(sums_ref)
    norm1 = total(later_ref[:, :128])
    beta = norm1 / total(sums_ref[:, :128])
    alpha1 = norm1 / (total(later_ref[:, 128:]) - beta * norm1 / alpha)
    for part in (0, 1):
        for at in range(0, r0_ref.shape[1], ROWS):
            span = (part, slice(at, at + ROWS))
            r0, r1 = r0_ref[span], r1_ref[span]
            step_ref[span] = alpha * r0 + alpha1 * (r1 + beta * r0)
            res_ref[span] = r1 - alpha1 * (acc_ref[span] + beta * q0_ref[span])


def call(
    kernel, name, out, operands, smem=0, scratch=(), flops=0, smem_out=False, hbm=0, vmem=28
):
    out_specs = [VMEM] * len(out)
    if smem_out:
        out_specs[-1] = SMEM
    cost = pl.CostEstimate(
        flops=flops,
        bytes_accessed=sum(x.size * x.dtype.itemsize for x in list(operands) + list(out)),
        transcendentals=0,
    )
    in_specs = [pl.BlockSpec(memory_space=pl.ANY)] * hbm + [SMEM] * smem
    return list(
        pl.pallas_call(
            kernel,
            out_shape=out,
            in_specs=in_specs + [VMEM] * (len(operands) - len(in_specs)),
            out_specs=out_specs,
            scratch_shapes=list(scratch),
            compiler_params=pltpu.CompilerParams(vmem_limit_bytes=vmem << 20),
            cost_estimate=cost,
            name=name,
        )(*operands)
    )


def shift(x, axis, by):
    size = lax.axis_size(axis)
    pairs = [(i, i + by) for i in range(size) if 0 <= i + by < size]
    return lax.ppermute(x, axis, pairs)


def exchange(x, axis, bit):
    return lax.ppermute(x, axis, [(i, i ^ bit) for i in range(lax.axis_size(axis))])


def halo_ty(edges):
    top, bottom, _, _ = edges
    return [shift(bottom, "ty", 1), shift(top, "ty", -1)]


def halo_tx(edges):
    _, _, left, right = edges
    return [shift(right, "tx", 1), shift(left, "tx", -1)]


def wait(x, done):
    return lax.optimization_barrier((x, done))


def all_bits(axis):
    return [1 << b for b in range(lax.axis_size(axis).bit_length() - 1)]


def positions(across):
    count = across.bit_length() - 1
    return [sum(((i >> b) & 1) << (count - 1 - b) for b in range(count)) for i in range(across)]


def sum_over(x, axis, bits):
    for bit in bits:
        x = x + exchange(x, axis, bit)
    return x


def scatter(low, high, bits, first=None, second=None):
    if first is not None:
        low, first = wait(low, first)
    x = (low + exchange(high, "tx", bits[0])).reshape((2,) * (len(bits) - 1) + low.shape[1:])
    for axis, bit in enumerate(bits[1:]):
        low, high = jnp.split(x, 2, axis)
        x = low + exchange(high, "tx", bit)
        if axis == 0 and second is not None:
            second, x = wait(second, x)
    return x, first, second


def gather(x, bits):
    shape = x.shape[-2:]
    for axis in range(len(bits) - 2, -1, -1):
        x = jnp.concatenate([x, exchange(x, "tx", bits[axis + 1])], axis)
    low = x.reshape((-1,) + shape)
    return low, exchange(low, "tx", bits[0])


def reduced(uppers, lowers, edges, finish):
    bits = all_bits("tx")
    other = [bits[1], bits[0]] + bits[2:]
    upper, halo, edges = scatter(uppers[0], uppers[1], bits, halo_ty(edges), edges)
    lower, _, _ = scatter(lowers[0], lowers[1], other, halo)
    halo = halo + halo_tx(edges)
    done, extra = finish(halo)
    if extra is not None:
        extra = extra.reshape(upper.shape[:-2] + extra.shape)
        upper = jnp.concatenate([upper, extra], -2)
    else:
        upper, done = wait(upper, done)
    return list(gather(upper, bits) + gather(lower, other)), done, halo


def on_device(spectrum, measured, pupil_mask, led_count, led_owner, led_offset):
    side = pupil_mask.shape[0]
    across = lax.axis_size("tx")
    part = across // 2
    slots = led_owner.shape[1]
    rows = side // 2
    tab = jnp.asarray(dft_tables(side))
    swap = np.zeros((side, side), np.float32)
    swap[np.arange(side), np.r_[0:side:2, 1:side:2]] = 1.0

    field_t = jax.ShapeDtypeStruct((part, 2, side, side), F32)
    pupil_t = jax.ShapeDtypeStruct((part, side, side), F32)
    q = part // 2
    low_t = jax.ShapeDtypeStruct((q, side - rows, side), F32)
    all_t = jax.ShapeDtypeStruct((part, side - rows, side), F32)
    far_t = [jax.ShapeDtypeStruct((part, rows, side), F32), low_t, low_t]
    near_t = [far_t[0], all_t, all_t]
    slot_t = jax.ShapeDtypeStruct((across, 4), jnp.int32)
    tile_t = jax.ShapeDtypeStruct(spectrum.shape, F32)
    sum_t = jax.ShapeDtypeStruct((8, 128), F32)
    pair_t = jax.ShapeDtypeStruct((8, 256), F32)
    row_t = jax.ShapeDtypeStruct((2, spectrum.shape[2]), F32)
    col_t = jax.ShapeDtypeStruct((2, spectrum.shape[1]), F32)
    edge_t = [row_t, row_t, col_t, col_t]
    cols_s = pltpu.VMEM((spectrum.shape[1], 8), F32)
    flops = part * 8 * 3 * side**3 * 2

    given = [
        led_count, led_owner.T, jnp.transpose(led_offset, (1, 2, 0)), spectrum, pupil_mask, tab,
    ]
    out = call(
        functools.partial(fields_kernel, False),
        "fields_far",
        far_t + [field_t, pupil_t] + edge_t + [slot_t],
        given,
        hbm=len(given),
        vmem=60,
        scratch=[
            (pltpu.SMEM if i < 3 else pltpu.VMEM)(x.shape, x.dtype) for i, x in enumerate(given)
        ]
        + [pltpu.SemaphoreType.DMA((len(given),))],
        flops=flops,
        smem_out=True,
    )
    far, (field_far, pupil_far), edges, slot = out[:3], out[3:5], out[5:9], out[9]
    out = call(
        functools.partial(fields_kernel, True),
        "fields_near",
        near_t + [field_t, pupil_t],
        [slot, led_owner.T, spectrum, pupil_mask, tab, measured, jnp.asarray(swap)] + far[1:],
        smem=1,
        flops=flops,
    )
    near, (field_near, pupil_near) = out[:3], out[3:]
    pupils, fields = [pupil_near, pupil_far], [field_near, field_far]

    def turn(sign, images, start):
        start = call(
            functools.partial(adjoint_kernel, slots),
            "adjoint",
            [tile_t],
            [slot, start, pupil_near, field_near, tab, images[0], images[2]],
            smem=1,
            flops=flops // 2,
        )[0]
        out = call(
            functools.partial(turn_kernel, slots, sign),
            "turn",
            [tile_t, sum_t] + edge_t,
            [slot, start, tab] + pupils + fields + images,
            smem=1,
            flops=3 * flops // 2,
        )
        return out[0], out[1], out[2:6]

    def linear(values, *before):
        far = call(
            functools.partial(linear_kernel, slots, False),
            "linear_far",
            far_t,
            [slot, values, tab, pupil_far, field_far] + list(before),
            smem=1,
            flops=flops,
        )
        near = call(
            functools.partial(linear_kernel, slots, True),
            "linear_near",
            near_t,
            [slot, values, tab, pupil_near, field_near] + far[1:],
            smem=1,
            flops=flops,
        )
        return [near[0], far[0]], near[1:]

    def bend(values, halo, norm=()):
        return call(
            bend_kernel, "bend", [tile_t, pair_t], [values] + halo + list(norm), scratch=[cols_s]
        )

    def norms(*operands):
        return call(
            functools.partial(norm_kernel, rows, len(operands) // 4),
            "norm",
            [pair_t],
            list(operands),
        )[0]

    first, second = all_bits("ty")[:1], all_bits("ty")[1:]
    images, bent, _ = reduced(
        [near[0], far[0]], near[1:], edges, lambda halo: (bend(spectrum, halo)[0], None)
    )
    r0, norm0, edges = turn(-1.0, images, bent)
    uppers, lowers = linear(r0)
    images0, bent, halo_r = reduced(
        uppers, lowers, edges, lambda halo: bend(r0, halo, [norm0])
    )

    sums = sum_over(norms(*images0), "ty", first)
    q0, _, edges = turn(1.0, images0, bent)
    uppers, lowers = linear(q0, sums)
    sums = sum_over(sums, "ty", second)
    uppers[1], sums = wait(uppers[1], sums)

    def residual(halo_q):
        r1, bent, later = call(
            residual_kernel,
            "residual",
            [tile_t, tile_t, pair_t],
            [r0, q0, sums] + halo_r + halo_q,
            scratch=[pltpu.VMEM(t.shape, F32) for t in edge_t] + [cols_s],
        )
        return (r1, bent), later

    images1, (r1, bent), _ = reduced(uppers, lowers, edges, residual)
    later = sum_over(norms(sums, *images0, *images1), "ty", first + second)

    acc = bent
    for near in (True, False):
        acc = call(
            functools.partial(last_kernel, slots, near),
            "last",
            [tile_t],
            [slot, acc, tab, sums] + pupils + fields + images0 + images1,
            smem=1,
            flops=flops // 2 if near else 3 * flops // 2,
        )[0]
    return tuple(
        call(finish_kernel, "finish", [tile_t, tile_t], [r0, r1, q0, acc, sums, later])
    )


def solution(mesh):
    placed = (P(None, "ty", "tx"), P(("ty", "tx"), None, None), P(), P(), P(), P())
    return jax.shard_map(
        on_device,
        mesh=mesh,
        in_specs=placed,
        out_specs=(P(None, "ty", "tx"), P(None, "ty", "tx")),
        check_vma=False,
    )
```

```python
import functools

import jax
import jax.numpy as jnp
import ml_dtypes
import numpy as np
from jax import lax
from jax.experimental import pallas as pl
from jax.experimental.pallas import tpu as pltpu
from jax.sharding import PartitionSpec as P

REG = 0.5
ROWS = 64
NEAR, FAR = ((0, 0),), ((0, 1), (1, 0), (1, 1))
F32 = jnp.float32
BF16 = jnp.bfloat16
VMEM = pl.BlockSpec(memory_space=pltpu.VMEM)
SMEM = pl.BlockSpec(memory_space=pltpu.SMEM)


def dft_tables(side):
    half = side // 2
    m = np.arange(half)[:, None]
    k = np.arange(half)[None, :]
    out = []
    for q in (0, 1):
        angle = 2 * np.pi * (((2 * m + q) * k) % side) / side
        cos, sin = np.cos(angle) / np.sqrt(side), np.sin(angle) / np.sqrt(side)
        mat = np.block([[cos.T, sin.T], [-sin.T, cos.T]])
        for each in (mat, mat.T):
            high = each.astype(ml_dtypes.bfloat16)
            low = (each - high.astype(np.float64)).astype(ml_dtypes.bfloat16)
            out += [high, low]
    return np.stack(out)


def split(x):
    high = x.astype(BF16)
    return high, (x - high.astype(F32)).astype(BF16)


def rmul(parts, tab_ref, at):
    a, b = parts
    high, low = tab_ref[at], tab_ref[at + 1]
    return jnp.dot(
        jnp.concatenate([a, b, a], 1),
        jnp.concatenate([high, high, low], 0),
        preferred_element_type=F32,
    )


def lmul(tab_ref, at, parts):
    a, b = parts
    high, low = tab_ref[at], tab_ref[at + 1]
    return jnp.dot(
        jnp.concatenate([high, high, low], 1),
        jnp.concatenate([a, b, a], 0),
        preferred_element_type=F32,
    )


def pipelined(count, stages):
    state = {}

    def run(stage, k):
        if k < count:
            state[k] = stages[stage](k, state.get(k))

    run(0, 0)
    run(1, 0)
    run(0, 1)
    for k in range(count):
        run(1, k + 1)
        run(2, k)
        run(3, k)
        run(0, k + 2)
        run(4, k)
        del state[k]


def masks(start, side):
    rows = lax.broadcasted_iota(jnp.int32, (side, side // 2), 0) >= start[0]
    lane = lax.broadcasted_iota(jnp.int32, (side, side // 2), 1)
    return rows, [lane + j * (side // 2) >= start[1] for j in (0, 1)]


def extract(v_ref, part, start, side):
    half = side // 2
    rows, cols = masks(start, side)
    out = []
    for j in (0, 1):
        near, far = slice(j * half, (j + 1) * half), slice(side + j * half, side + (j + 1) * half)
        top = jnp.where(cols[j], v_ref[part, :side, near], v_ref[part, :side, far])
        low = jnp.where(cols[j], v_ref[part, side:, near], v_ref[part, side:, far])
        out.append(jnp.where(rows, top, low))
    return out


def deposit(acc_ref, part, start, halves, side):
    half = side // 2
    rows, cols = masks(start, side)
    for j, x in enumerate(halves):
        top, low = jnp.where(rows, x, 0.0), jnp.where(rows, 0.0, x)
        for at, value in ((slice(0, side), top), (slice(side, 2 * side), low)):
            near = (part, at, slice(j * half, (j + 1) * half))
            far = (part, at, slice(side + j * half, side + (j + 1) * half))
            acc_ref[near] = acc_ref[near] + jnp.where(cols[j], value, 0.0)
            acc_ref[far] = acc_ref[far] + jnp.where(cols[j], 0.0, value)


def to_images(jobs, v_ref, tab_ref):
    def cut(k, _):
        pupil, start, _ = jobs[k]
        pupil, start = pupil(), start()
        side = pupil.shape[0]
        half = side // 2
        plus, minus = [], []
        for part in (0, 1):
            x0, x1 = extract(v_ref, part, start, side)
            x0, x1 = x0 * pupil[:, :half], x1 * pupil[:, half:]
            plus.append(x0 + x1)
            minus.append(x0 - x1)
        return split(jnp.concatenate(plus, 1)), split(jnp.concatenate(minus, 1))

    def columns(k, x):
        return rmul(x[0], tab_ref, 0), rmul(x[1], tab_ref, 4)

    def fold(k, x):
        even, odd = x
        half = even.shape[1] // 2
        re = jnp.concatenate([even[:, :half], odd[:, :half]], 1)
        im = jnp.concatenate([even[:, half:], odd[:, half:]], 1)
        top = jnp.concatenate([re[:half] + re[half:], im[:half] + im[half:]], 0)
        low = jnp.concatenate([re[:half] - re[half:], im[:half] - im[half:]], 0)
        return split(top), split(low)

    def rows(k, x):
        return lmul(tab_ref, 2, x[0]), lmul(tab_ref, 6, x[1])

    def give(k, x):
        even, odd = x
        half = even.shape[0] // 2
        jobs[k][2](
            jnp.concatenate([even[:half], odd[:half]], 0),
            jnp.concatenate([even[half:], odd[half:]], 0),
        )

    pipelined(len(jobs), (cut, columns, fold, rows, give))


def from_images(jobs, acc_ref, tab_ref):
    def cut(k, _):
        re, im = jobs[k][2]()
        half = re.shape[0] // 2
        even = jnp.concatenate([re[:half], im[:half]], 0)
        odd = jnp.concatenate([re[half:], im[half:]], 0)
        return split(even), split(odd)

    def rows(k, x):
        return lmul(tab_ref, 0, x[0]), lmul(tab_ref, 4, x[1])

    def fold(k, x):
        even, odd = x
        half = even.shape[0] // 2
        top, low = even + odd, even - odd
        re = jnp.concatenate([top[:half], low[:half]], 0)
        im = jnp.concatenate([top[half:], low[half:]], 0)
        return (
            split(jnp.concatenate([re[:, :half], im[:, :half]], 1)),
            split(jnp.concatenate([re[:, half:], im[:, half:]], 1)),
        )

    def columns(k, x):
        return rmul(x[0], tab_ref, 2), rmul(x[1], tab_ref, 6)

    def give(k, x):
        even, odd = x
        pupil, start = jobs[k][0](), jobs[k][1]()
        half = pupil.shape[0] // 2
        p0, p1 = pupil[:, :half], pupil[:, half:]
        left, right = even + odd, even - odd
        for part in (0, 1):
            at = slice(part * half, (part + 1) * half)
            deposit(acc_ref, part, start, (left[:, at] * p0, right[:, at] * p1), 2 * half)

    pipelined(len(jobs), (cut, rows, fold, columns, give))


def where(slot_ref, i):
    return lambda: (slot_ref[i, 0], slot_ref[i, 1])


def tiles(x):
    rows, cols = x.shape
    x = jnp.sum(x.reshape(rows // 8, 8, cols), 0)
    return sum(x[:, i * 128 : (i + 1) * 128] for i in range(cols // 128))


def total(tile):
    return jnp.sum(jnp.sum(tile, 0, keepdims=True), 1, keepdims=True)


def side_columns(left_ref, right_ref, cols_ref):
    size = left_ref.shape[1]
    rows = jnp.concatenate([left_ref[...], right_ref[...], jnp.zeros((4, size), F32)], 0)
    cols_ref[...] = jnp.transpose(rows)


def laplace_rows(v_ref, halo, cols_ref, part, at, count):
    top_ref, bottom_ref = halo[:2]
    rows, cols = v_ref.shape[1:]
    here = v_ref[part, at : at + count, :]
    up = (
        jnp.concatenate([top_ref[part : part + 1, :], v_ref[part, : count - 1, :]], 0)
        if at == 0
        else v_ref[part, at - 1 : at + count - 1, :]
    )
    down = (
        jnp.concatenate([v_ref[part, at + 1 :, :], bottom_ref[part : part + 1, :]], 0)
        if at + count == rows
        else v_ref[part, at + 1 : at + count + 1, :]
    )
    lane = lax.broadcasted_iota(jnp.int32, (count, cols), 1)
    span = slice(at, at + count)
    before = jnp.where(lane == 0, cols_ref[span, part : part + 1], pltpu.roll(here, 1, 1))
    after = jnp.where(
        lane == cols - 1, cols_ref[span, 2 + part : 3 + part], pltpu.roll(here, cols - 1, 1)
    )
    return here, 4.0 * here - (up + down + before + after)


def write_edges(v_ref, edges):
    rows, cols = v_ref.shape[1:]
    low = [lax.rem(lax.axis_index(axis), 2) == 0 for axis in ("ty", "tx")]
    for part in (0, 1):
        one = slice(part, part + 1)
        left = jnp.transpose(v_ref[part, :, :128])[:1]
        right = jnp.transpose(v_ref[part, :, cols - 128 :])[127:128]
        top, bottom = v_ref[part, 0:1, :], v_ref[part, rows - 1 : rows, :]
        edges[0][one, :] = jnp.where(low[0], bottom, top)
        edges[1][one, :] = jnp.where(low[0], top, bottom)
        edges[2][one, :] = jnp.where(low[1], right, left)
        edges[3][one, :] = jnp.where(low[1], left, right)


def read_halo(came, halo):
    for axis, name in enumerate(("ty", "tx")):
        low = lax.rem(lax.axis_index(name), 2) == 0
        a, b = came[2 * axis][...], came[2 * axis + 1][...]
        halo[2 * axis][...] = jnp.where(low, b, a)
        halo[2 * axis + 1][...] = jnp.where(low, a, b)


def unpack(refs, *counts):
    out = []
    for count in counts:
        out.append(refs[0] if count is None else refs[:count])
        refs = refs[1 if count is None else count :]
    assert not refs
    return out


def find_slots(count_ref, owner_ref, offset_ref, slot_ref):
    slots = owner_ref.shape[0]
    across = lax.axis_size("tx")
    row_start = lax.axis_index("ty") * across
    column = lax.axis_index("tx")
    order = positions(across)
    for i in range(across):
        capture = row_start + jnp.bitwise_xor(column, order[i])
        row = col = live = jnp.int32(0)
        for t in range(slots):
            hit = jnp.where((owner_ref[t, capture] == column) & (t < count_ref[capture]), 1, 0)
            row += hit * offset_ref[t, 0, capture]
            col += hit * offset_ref[t, 1, capture]
            live += hit
        slot_ref[i, 0] = row
        slot_ref[i, 1] = col
        slot_ref[i, 2] = live


def fields_kernel(*refs):
    given, results, edges, slot_ref, kept, made, sems = unpack(refs, 8, 8, 4, None, 8, 8, None)
    uppers, lowers, fields, pupils = unpack(made, 2, 2, 2, 2)
    copies = [pltpu.make_async_copy(a, b, sems.at[i]) for i, (a, b) in enumerate(zip(given, kept))]
    for copy in copies:
        copy.start()
    for copy in copies[:3]:
        copy.wait()
    count_ref, owner_ref, offset_ref, v_ref, mask_ref, tab_ref, measured_ref, swap_ref = kept
    slots, across = owner_ref.shape[0], lax.axis_size("tx")
    find_slots(count_ref, owner_ref, offset_ref, slot_ref)
    for copy in copies[3:]:
        copy.wait()
    assert len(copies) == len(given)
    part = across // 2
    count = part // 2
    rows = uppers[0].shape[1]
    mask = mask_ref[...].astype(F32)
    side = mask.shape[0]
    highest = lax.Precision.HIGHEST
    swap = swap_ref[...]
    image = jnp.dot(swap, measured_ref[0], precision=highest, preferred_element_type=F32)
    data = lax.dot_general(
        image, swap, (((1,), (1,)), ((), ())), precision=highest, preferred_element_type=F32
    )
    jobs = []
    for y, z, i in groups(count):
        at, base = z * count + i, y * part + z * count + i

        def pupil(y=y, at=at, base=base):
            x = pltpu.roll(mask, lax.rem(slot_ref[base, 0], side), 0)
            x = pltpu.roll(x, lax.rem(slot_ref[base, 1], side), 1)
            pupils[y][at] = x
            return x

        def take(re, im, y=y, z=z, i=i, at=at, base=base):
            live = slot_ref[base, 2].astype(F32)
            re, im = re * live, im * live
            fields[y][at, 0] = 2.0 * re
            fields[y][at, 1] = 2.0 * im
            image = re * re + im * im
            if base == 0:
                image = image - data
            uppers[y][at] = image[:rows]
            lowers[z][y * count + i] = image[rows:]
            for k, j in ((y, at), (2 + z, y * count + i), (4 + y, at), (6 + y, at)):
                copy = pltpu.make_async_copy(made[k].at[j], results[k].at[j], sems.at[len(copies)])
                copy.start()
                copies.append(copy)

        jobs.append((pupil, where(slot_ref, base), take))
    to_images(jobs, v_ref, tab_ref)
    write_edges(v_ref, edges)
    for copy in copies[len(given) :]:
        copy.wait()


def groups(count):
    return [(y, z, i) for y, z in ((1, 0), (1, 1), (0, 1), (0, 0)) for i in range(count)]


def deposit_images(which, slot_ref, image_at, fields, pupils, tab_ref, acc_ref):
    count = fields[0].shape[0] // 2
    jobs = []
    for y, z, i in [(y, z, i) for y, z in which for i in range(count)]:
        at = z * count + i

        def images(y=y, z=z, i=i, at=at):
            image = image_at(y, z, i)
            return fields[y][at, 0] * image, fields[y][at, 1] * image

        def pupil(y=y, at=at):
            return pupils[y][at]

        jobs.append((pupil, where(slot_ref, 2 * y * count + at), images))
    from_images(jobs, acc_ref, tab_ref)


def linear_kernel(slot_ref, v_ref, tab_ref, *refs):
    pupils, fields, uppers, lowers = refs[:2], refs[2:4], refs[-4:-2], refs[-2:]
    count = fields[0].shape[0] // 2
    rows = uppers[0].shape[1]
    jobs = []
    for y, z, i in groups(count):
        at = z * count + i

        def take(re, im, y=y, z=z, i=i, at=at):
            image = fields[y][at, 0] * re + fields[y][at, 1] * im
            uppers[y][at] = image[:rows]
            lowers[z][y * count + i] = image[rows:]

        def pupil(y=y, at=at):
            return pupils[y][at]

        jobs.append((pupil, where(slot_ref, 2 * y * count + at), take))
    to_images(jobs, v_ref, tab_ref)


def one_image(firsts, seconds, count):
    rows = firsts[0].shape[2] - firsts[0].shape[1]

    def image(y, z, i):
        return jnp.concatenate(
            [firsts[y][z * count + i], seconds[z][y * count + i, :rows, :]], 0
        )

    return image


def adjoint_kernel(slot_ref, start_ref, tab_ref, *refs):
    pupils, fields, firsts, seconds, acc_ref = unpack(refs, 2, 2, 2, 2, None)
    acc_ref[...] = start_ref[...]
    image = one_image(firsts, seconds, fields[0].shape[0] // 2)
    deposit_images(NEAR, slot_ref, image, fields, pupils, tab_ref, acc_ref)


def turn_kernel(sign, slot_ref, part_ref, tab_ref, *refs):
    pupils, fields, firsts, seconds, (out_ref, sum_ref), edges = unpack(refs, 2, 2, 2, 2, 2, 4)
    out_ref[...] = part_ref[...]
    image = one_image(firsts, seconds, fields[0].shape[0] // 2)
    deposit_images(FAR, slot_ref, image, fields, pupils, tab_ref, out_ref)
    found = jnp.zeros((8, 128), F32)
    if sign < 0:
        for part in (0, 1):
            for at in range(0, out_ref.shape[1], ROWS):
                value = -out_ref[part, at : at + ROWS, :]
                out_ref[part, at : at + ROWS, :] = value
                found += tiles(value * value)
    sum_ref[...] = found
    write_edges(out_ref, edges)


def bend_kernel(v_ref, *refs):
    came, refs = refs[:4], refs[4:]
    norm_ref, refs = (refs[0], refs[1:]) if len(refs) == 8 else (None, refs)
    (bent_ref, sums_ref), halo, cols_ref = unpack(refs, 2, 4, None)
    read_halo(came, halo)
    side_columns(halo[2], halo[3], cols_ref)
    found = jnp.zeros((8, 128), F32)
    for part in (0, 1):
        for at in range(0, v_ref.shape[1], ROWS):
            here, bent = laplace_rows(v_ref, halo, cols_ref, part, at, ROWS)
            bent = REG * bent
            bent_ref[part, at : at + ROWS, :] = bent
            found += tiles(here * bent)
    sums_ref[:, 128:] = found
    sums_ref[:, :128] = found if norm_ref is None else norm_ref[...]


def step_size(sums_ref):
    return total(sums_ref[:, :128]) / total(sums_ref[:, 128:])


def residual_kernel(r0_ref, q0_ref, sums_ref, *refs):
    halo_r, halo_q, (r1_ref, bent_ref, found_ref), halo, cols_ref = unpack(refs, 4, 4, 3, 4, None)
    alpha = step_size(sums_ref)
    read_halo([a[...] - alpha * b[...] for a, b in zip(halo_r, halo_q)], halo)
    side_columns(halo[2], halo[3], cols_ref)
    sums = [jnp.zeros((8, 128), F32) for _ in range(2)]
    for part in (0, 1):
        for at in range(0, r0_ref.shape[1], ROWS):
            span = slice(at, at + ROWS)
            r1_ref[part, span, :] = r0_ref[part, span, :] - alpha * q0_ref[part, span, :]
        for at in range(0, r0_ref.shape[1], ROWS):
            span = slice(at, at + ROWS)
            here, bent = laplace_rows(r1_ref, halo, cols_ref, part, at, ROWS)
            bent = REG * bent
            bent_ref[part, span, :] = bent
            sums[0] += tiles(here * here)
            sums[1] += tiles(here * bent)
    found_ref[:, :128] = sums[0]
    found_ref[:, 128:] = sums[1]


def last_kernel(which, slot_ref, start_ref, tab_ref, sums_ref, *refs):
    pupils, fields, first0, second0, firstq, secondq, acc_ref = unpack(
        refs, 2, 2, 2, 2, 2, 2, None
    )
    acc_ref[...] = start_ref[...]
    alpha = step_size(sums_ref)
    count = fields[0].shape[0] // 2
    a, b = one_image(first0, second0, count), one_image(firstq, secondq, count)
    deposit_images(
        which, slot_ref, lambda *at: a(*at) - alpha * b(*at), fields, pupils, tab_ref, acc_ref
    )


def norm_kernel(rows, count, *refs):
    sums_ref, refs = (refs[0], refs[1:]) if count == 2 else (None, refs)
    w0, refs = refs[:4], refs[4:]
    wq, out_ref = (refs[:4], refs[4]) if count == 2 else (None, refs[0])
    alpha = step_size(sums_ref) if count == 2 else None

    def body(i, acc):
        for j in range(4):
            w = w0[j][i] if j < 2 else w0[j][i, :rows, :]
            if wq:
                w = w - alpha * (wq[j][i] if j < 2 else wq[j][i, :rows, :])
            acc += tiles(w * w)
        return acc

    part = w0[0].shape[0]
    squares = lax.fori_loop(0, part, body, jnp.zeros((8, 128), F32))
    came = jnp.zeros((8, 256), F32)
    for ref in (wq or w0)[2:]:
        for i in range(part):
            came += ref[i, rows:, :]
    out_ref[:, :128] = came[:, :128]
    out_ref[:, 128:] = came[:, 128:] + squares


def finish_kernel(r0_ref, r1_ref, q0_ref, acc_ref, sums_ref, later_ref, *refs):
    results, made, sems = unpack(refs, 2, 2, None)
    step_ref, res_ref = made
    alpha = step_size(sums_ref)
    norm1 = total(later_ref[:, :128])
    beta = norm1 / total(sums_ref[:, :128])
    alpha1 = norm1 / (total(later_ref[:, 128:]) - beta * norm1 / alpha)
    copies = []
    for part in (0, 1):
        for at in range(0, r0_ref.shape[1], ROWS):
            span = (part, slice(at, at + ROWS))
            r0, r1 = r0_ref[span], r1_ref[span]
            step_ref[span] = alpha * r0 + alpha1 * (r1 + beta * r0)
            res_ref[span] = r1 - alpha1 * (acc_ref[span] + beta * q0_ref[span])
            for k in (0, 1):
                copy = pltpu.make_async_copy(
                    made[k].at[part, pl.ds(at, ROWS)],
                    results[k].at[part, pl.ds(at, ROWS)],
                    sems.at[len(copies)],
                )
                copy.start()
                copies.append(copy)
    for copy in copies:
        copy.wait()


def call(
    kernel, name, out, operands, smem=0, scratch=(), flops=0, smem_out=False, hbm=0, hbm_out=0,
    vmem=28,
):
    out_specs = [pl.BlockSpec(memory_space=pl.ANY)] * hbm_out + [VMEM] * (len(out) - hbm_out)
    if smem_out:
        out_specs[-1] = SMEM
    cost = pl.CostEstimate(
        flops=flops,
        bytes_accessed=sum(x.size * x.dtype.itemsize for x in list(operands) + list(out)),
        transcendentals=0,
    )
    in_specs = [pl.BlockSpec(memory_space=pl.ANY)] * hbm + [SMEM] * smem
    return list(
        pl.pallas_call(
            kernel,
            out_shape=out,
            in_specs=in_specs + [VMEM] * (len(operands) - len(in_specs)),
            out_specs=out_specs,
            scratch_shapes=list(scratch),
            compiler_params=pltpu.CompilerParams(vmem_limit_bytes=vmem << 20),
            cost_estimate=cost,
            name=name,
        )(*operands)
    )


def shift(x, axis, by):
    size = lax.axis_size(axis)
    pairs = [(i, i + by) for i in range(size) if 0 <= i + by < size]
    return lax.ppermute(x, axis, pairs)


def exchange(x, axis, bit):
    return lax.ppermute(x, axis, [(i, i ^ bit) for i in range(lax.axis_size(axis))])


def swap_edges(edges, axis):
    size = lax.axis_size(axis)
    out = []
    for begin, edge in enumerate(edges):
        pairs = [(i, i + 1) for i in range(begin, size - 1, 2)]
        out.append(lax.ppermute(edge, axis, pairs + [(j, i) for i, j in pairs]))
    return out


def wait(x, done):
    return lax.optimization_barrier((x, done))


def all_bits(axis):
    return [1 << b for b in range(lax.axis_size(axis).bit_length() - 1)]


def positions(across):
    count = across.bit_length() - 1
    return [sum(((i >> b) & 1) << (count - 1 - b) for b in range(count)) for i in range(across)]


def sum_over(x, axis, bits):
    for bit in bits:
        x = x + exchange(x, axis, bit)
    return x


def scatter(low, high, bits, first, second):
    low, first = wait(low, first)
    x = (low + exchange(high, "tx", bits[0])).reshape((2,) * (len(bits) - 1) + low.shape[1:])
    for axis, bit in enumerate(bits[1:]):
        low, high = jnp.split(x, 2, axis)
        if axis == 0:
            low, second = wait(low, second)
        x = low + exchange(high, "tx", bit)
    return x, first, second


def gather(x, bits):
    shape = x.shape[-2:]
    for axis in range(len(bits) - 2, -1, -1):
        x = jnp.concatenate([x, exchange(x, "tx", bits[axis + 1])], axis)
    low = x.reshape((-1,) + shape)
    return low, exchange(low, "tx", bits[0])


def reduced(uppers, lowers, edges, finish):
    bits = all_bits("tx")
    other = [bits[1], bits[0]] + bits[2:]
    upper, first, second = scatter(
        uppers[0], uppers[1], bits, swap_edges(edges[:2], "ty"), swap_edges(edges[2:], "tx")
    )
    lower, first, second = scatter(lowers[0], lowers[1], other, first, second)
    halo = first + second
    done, extra = finish(halo)
    if extra is not None:
        extra = extra.reshape(lower.shape[:-2] + extra.shape)
        lower = jnp.concatenate([lower, extra], -2)
    else:
        lower, done = wait(lower, done)
    return list(gather(upper, bits) + gather(lower, other)), done, halo


def on_device(spectrum, measured, pupil_mask, led_count, led_owner, led_offset):
    side = pupil_mask.shape[0]
    across = lax.axis_size("tx")
    part = across // 2
    slots = led_owner.shape[1]
    rows = side // 2
    tab = jnp.asarray(dft_tables(side))
    swap = np.zeros((side, side), np.float32)
    swap[np.arange(side), np.r_[0:side:2, 1:side:2]] = 1.0

    field_t = jax.ShapeDtypeStruct((part, 2, side, side), F32)
    pupil_t = jax.ShapeDtypeStruct((part, side, side), F32)
    image_t = [jax.ShapeDtypeStruct((part, n, side), F32) for n in (rows, side - rows)]
    slot_t = jax.ShapeDtypeStruct((across, 4), jnp.int32)
    tile_t = jax.ShapeDtypeStruct(spectrum.shape, F32)
    sum_t = jax.ShapeDtypeStruct((8, 128), F32)
    pair_t = jax.ShapeDtypeStruct((8, 256), F32)
    row_t = jax.ShapeDtypeStruct((2, spectrum.shape[2]), F32)
    col_t = jax.ShapeDtypeStruct((2, spectrum.shape[1]), F32)
    edge_t = [row_t, row_t, col_t, col_t]
    cols_s = pltpu.VMEM((spectrum.shape[1], 8), F32)
    flops = part * 8 * 3 * side**3 * 2

    given = [
        led_count, led_owner.T, jnp.transpose(led_offset, (1, 2, 0)), spectrum, pupil_mask, tab,
        measured, jnp.asarray(swap),
    ]
    made = [image_t[0]] * 2 + [image_t[1]] * 2 + [field_t] * 2 + [pupil_t] * 2
    out = call(
        fields_kernel,
        "fields",
        made + edge_t + [slot_t],
        given,
        hbm=len(given),
        hbm_out=len(made),
        vmem=60,
        scratch=[
            (pltpu.SMEM if i < 3 else pltpu.VMEM)(x.shape, x.dtype) for i, x in enumerate(given)
        ]
        + [pltpu.VMEM(t.shape, t.dtype) for t in made]
        + [pltpu.SemaphoreType.DMA((len(given) + 4 * across,))],
        flops=2 * flops,
        smem_out=True,
    )
    uppers, lowers, fields, pupils, edges, slot = (
        out[:2], out[2:4], out[4:6], out[6:8], out[8:12], out[12],
    )

    def adjoint(images, start):
        return call(
            adjoint_kernel,
            "adjoint",
            [tile_t],
            [slot, start, tab] + pupils + fields + [images[0], images[0], images[2], images[2]],
            smem=1,
            flops=flops // 2,
        )[0]

    def turn(sign, images, start):
        out = call(
            functools.partial(turn_kernel, sign),
            "turn",
            [tile_t, sum_t] + edge_t,
            [slot, start, tab] + pupils + fields + images,
            smem=1,
            flops=3 * flops // 2,
        )
        return out[0], out[1], out[2:6]

    def linear(values, *before):
        out = call(
            linear_kernel,
            "linear",
            [image_t[0]] * 2 + [image_t[1]] * 2,
            [slot, values, tab] + pupils + fields + list(before),
            smem=1,
            flops=2 * flops,
        )
        return out[:2], out[2:]

    def bend(values, halo, norm=()):
        return call(
            bend_kernel,
            "bend",
            [tile_t, pair_t],
            [values] + halo + list(norm),
            scratch=[pltpu.VMEM(t.shape, F32) for t in edge_t] + [cols_s],
        )

    def norms(*operands):
        return call(
            functools.partial(norm_kernel, side - rows, len(operands) // 4),
            "norm",
            [pair_t],
            list(operands),
        )[0]

    first, second = all_bits("ty")[:1], all_bits("ty")[1:]
    images, bent, _ = reduced(
        uppers, lowers, edges, lambda halo: (bend(spectrum, halo)[0], None)
    )
    r0, norm0, edges = turn(-1.0, images, adjoint(images, bent))
    uppers, lowers = linear(r0)
    images0, bent, halo_r = reduced(
        uppers, lowers, edges, lambda halo: bend(r0, halo, [norm0])
    )

    start = adjoint(images0, bent)
    waited, start = wait(images0, start)
    sums = sum_over(norms(*waited), "ty", first)
    q0, _, edges = turn(1.0, images0, start)
    uppers, lowers = linear(q0, sums)
    sums = sum_over(sums, "ty", second)
    (uppers[1], lowers[1]), sums = wait((uppers[1], lowers[1]), sums)

    def residual(halo_q):
        r1, bent, later = call(
            residual_kernel,
            "residual",
            [tile_t, tile_t, pair_t],
            [r0, q0, sums] + halo_r + halo_q,
            scratch=[pltpu.VMEM(t.shape, F32) for t in edge_t] + [cols_s],
        )
        return (r1, bent), later

    images1, (r1, bent), _ = reduced(uppers, lowers, edges, residual)
    def last(which, acc, w0, wq):
        return call(
            functools.partial(last_kernel, which),
            "last",
            [tile_t],
            [slot, acc, tab, sums] + pupils + fields + w0 + wq,
            smem=1,
            flops=len(which) * flops // 2,
        )[0]

    early0, early1 = [[w[0], w[0], w[2], w[2]] for w in (images0, images1)]
    acc = last(NEAR, bent, early0, early1)
    waited, acc = wait(images1, acc)
    later = sum_over(norms(sums, *images0, *waited), "ty", first + second)
    acc = last(FAR[:2], acc, images0, images1)
    acc = last(FAR[2:], acc, images0, images1)
    return tuple(
        call(
            finish_kernel,
            "finish",
            [tile_t, tile_t],
            [r0, r1, q0, acc, sums, later],
            hbm_out=2,
            scratch=[
                pltpu.VMEM(tile_t.shape, F32),
                pltpu.VMEM(tile_t.shape, F32),
                pltpu.SemaphoreType.DMA((4 * (spectrum.shape[1] // ROWS),)),
            ],
        )
    )


def solution(mesh):
    placed = (P(None, "ty", "tx"), P(("ty", "tx"), None, None), P(), P(), P(), P())
    return jax.shard_map(
        on_device,
        mesh=mesh,
        in_specs=placed,
        out_specs=(P(None, "ty", "tx"), P(None, "ty", "tx")),
        check_vma=False,
    )
```

```python
import functools

import jax
import jax.numpy as jnp
import ml_dtypes
import numpy as np
from jax import lax
from jax.experimental import pallas as pl
from jax.experimental.pallas import tpu as pltpu
from jax.sharding import PartitionSpec as P

REG = 0.5
ROWS = 64
NEAR, FAR = ((0, 0),), ((0, 1), (1, 0), (1, 1))
F32 = jnp.float32
BF16 = jnp.bfloat16
VMEM = pl.BlockSpec(memory_space=pltpu.VMEM)
SMEM = pl.BlockSpec(memory_space=pltpu.SMEM)


def dft_tables(side):
    half = side // 2
    m = np.arange(half)[:, None]
    k = np.arange(half)[None, :]
    out = []
    for q in (0, 1):
        angle = 2 * np.pi * (((2 * m + q) * k) % side) / side
        cos, sin = np.cos(angle) / np.sqrt(side), np.sin(angle) / np.sqrt(side)
        mat = np.block([[cos.T, sin.T], [-sin.T, cos.T]])
        for each in (mat, mat.T):
            high = each.astype(ml_dtypes.bfloat16)
            low = (each - high.astype(np.float64)).astype(ml_dtypes.bfloat16)
            out += [high, low]
    return np.stack(out)


def split(x):
    high = x.astype(BF16)
    return high, (x - high.astype(F32)).astype(BF16)


def rmul(parts, tab_ref, at):
    a, b = parts
    high, low = tab_ref[at], tab_ref[at + 1]
    return jnp.dot(
        jnp.concatenate([a, b, a], 1),
        jnp.concatenate([high, high, low], 0),
        preferred_element_type=F32,
    )


def lmul(tab_ref, at, parts):
    a, b = parts
    high, low = tab_ref[at], tab_ref[at + 1]
    return jnp.dot(
        jnp.concatenate([high, high, low], 1),
        jnp.concatenate([a, b, a], 0),
        preferred_element_type=F32,
    )


def pipelined(count, stages):
    state = {}

    def run(stage, k):
        if k < count:
            state[k] = stages[stage](k, state.get(k))

    run(0, 0)
    run(1, 0)
    run(0, 1)
    for k in range(count):
        run(1, k + 1)
        run(2, k)
        run(3, k)
        run(0, k + 2)
        run(4, k)
        del state[k]


def masks(start, side):
    rows = lax.broadcasted_iota(jnp.int32, (side, side // 2), 0) >= start[0]
    lane = lax.broadcasted_iota(jnp.int32, (side, side // 2), 1)
    return rows, [lane + j * (side // 2) >= start[1] for j in (0, 1)]


def extract(v_ref, part, start, side):
    half = side // 2
    rows, cols = masks(start, side)
    out = []
    for j in (0, 1):
        near, far = slice(j * half, (j + 1) * half), slice(side + j * half, side + (j + 1) * half)
        top = jnp.where(cols[j], v_ref[part, :side, near], v_ref[part, :side, far])
        low = jnp.where(cols[j], v_ref[part, side:, near], v_ref[part, side:, far])
        out.append(jnp.where(rows, top, low))
    return out


def deposit(acc_ref, part, start, halves, side):
    half = side // 2
    rows, cols = masks(start, side)
    for j, x in enumerate(halves):
        top, low = jnp.where(rows, x, 0.0), jnp.where(rows, 0.0, x)
        for at, value in ((slice(0, side), top), (slice(side, 2 * side), low)):
            near = (part, at, slice(j * half, (j + 1) * half))
            far = (part, at, slice(side + j * half, side + (j + 1) * half))
            acc_ref[near] = acc_ref[near] + jnp.where(cols[j], value, 0.0)
            acc_ref[far] = acc_ref[far] + jnp.where(cols[j], 0.0, value)


def to_images(jobs, v_ref, tab_ref):
    def cut(k, _):
        pupil, start, _ = jobs[k]
        pupil, start = pupil(), start()
        side = pupil.shape[0]
        half = side // 2
        plus, minus = [], []
        for part in (0, 1):
            x0, x1 = extract(v_ref, part, start, side)
            x0, x1 = x0 * pupil[:, :half], x1 * pupil[:, half:]
            plus.append(x0 + x1)
            minus.append(x0 - x1)
        return split(jnp.concatenate(plus, 1)), split(jnp.concatenate(minus, 1))

    def columns(k, x):
        return rmul(x[0], tab_ref, 0), rmul(x[1], tab_ref, 4)

    def fold(k, x):
        even, odd = x
        half = even.shape[1] // 2
        re = jnp.concatenate([even[:, :half], odd[:, :half]], 1)
        im = jnp.concatenate([even[:, half:], odd[:, half:]], 1)
        top = jnp.concatenate([re[:half] + re[half:], im[:half] + im[half:]], 0)
        low = jnp.concatenate([re[:half] - re[half:], im[:half] - im[half:]], 0)
        return split(top), split(low)

    def rows(k, x):
        return lmul(tab_ref, 2, x[0]), lmul(tab_ref, 6, x[1])

    def give(k, x):
        even, odd = x
        half = even.shape[0] // 2
        jobs[k][2](
            jnp.concatenate([even[:half], odd[:half]], 0),
            jnp.concatenate([even[half:], odd[half:]], 0),
        )

    pipelined(len(jobs), (cut, columns, fold, rows, give))


def from_images(jobs, acc_ref, tab_ref):
    def cut(k, _):
        re, im = jobs[k][2]()
        half = re.shape[0] // 2
        even = jnp.concatenate([re[:half], im[:half]], 0)
        odd = jnp.concatenate([re[half:], im[half:]], 0)
        return split(even), split(odd)

    def rows(k, x):
        return lmul(tab_ref, 0, x[0]), lmul(tab_ref, 4, x[1])

    def fold(k, x):
        even, odd = x
        half = even.shape[0] // 2
        top, low = even + odd, even - odd
        re = jnp.concatenate([top[:half], low[:half]], 0)
        im = jnp.concatenate([top[half:], low[half:]], 0)
        return (
            split(jnp.concatenate([re[:, :half], im[:, :half]], 1)),
            split(jnp.concatenate([re[:, half:], im[:, half:]], 1)),
        )

    def columns(k, x):
        return rmul(x[0], tab_ref, 2), rmul(x[1], tab_ref, 6)

    def give(k, x):
        even, odd = x
        pupil, start = jobs[k][0](), jobs[k][1]()
        half = pupil.shape[0] // 2
        p0, p1 = pupil[:, :half], pupil[:, half:]
        left, right = even + odd, even - odd
        for part in (0, 1):
            at = slice(part * half, (part + 1) * half)
            deposit(acc_ref, part, start, (left[:, at] * p0, right[:, at] * p1), 2 * half)

    pipelined(len(jobs), (cut, rows, fold, columns, give))


def where(slot_ref, i):
    return lambda: (slot_ref[i, 0], slot_ref[i, 1])


def tiles(x):
    rows, cols = x.shape
    x = jnp.sum(x.reshape(rows // 8, 8, cols), 0)
    return sum(x[:, i * 128 : (i + 1) * 128] for i in range(cols // 128))


def total(tile):
    return jnp.sum(jnp.sum(tile, 0, keepdims=True), 1, keepdims=True)


def side_columns(left_ref, right_ref, cols_ref):
    size = left_ref.shape[1]
    rows = jnp.concatenate([left_ref[...], right_ref[...], jnp.zeros((4, size), F32)], 0)
    cols_ref[...] = jnp.transpose(rows)


def laplace_rows(v_ref, halo, cols_ref, part, at, count):
    top_ref, bottom_ref = halo[:2]
    rows, cols = v_ref.shape[1:]
    here = v_ref[part, at : at + count, :]
    up = (
        jnp.concatenate([top_ref[part : part + 1, :], v_ref[part, : count - 1, :]], 0)
        if at == 0
        else v_ref[part, at - 1 : at + count - 1, :]
    )
    down = (
        jnp.concatenate([v_ref[part, at + 1 :, :], bottom_ref[part : part + 1, :]], 0)
        if at + count == rows
        else v_ref[part, at + 1 : at + count + 1, :]
    )
    lane = lax.broadcasted_iota(jnp.int32, (count, cols), 1)
    span = slice(at, at + count)
    before = jnp.where(lane == 0, cols_ref[span, part : part + 1], pltpu.roll(here, 1, 1))
    after = jnp.where(
        lane == cols - 1, cols_ref[span, 2 + part : 3 + part], pltpu.roll(here, cols - 1, 1)
    )
    return here, 4.0 * here - (up + down + before + after)


def write_edges(v_ref, edges):
    rows, cols = v_ref.shape[1:]
    low = [lax.rem(lax.axis_index(axis), 2) == 0 for axis in ("ty", "tx")]
    for part in (0, 1):
        one = slice(part, part + 1)
        left = jnp.transpose(v_ref[part, :, :128])[:1]
        right = jnp.transpose(v_ref[part, :, cols - 128 :])[127:128]
        top, bottom = v_ref[part, 0:1, :], v_ref[part, rows - 1 : rows, :]
        edges[0][one, :] = jnp.where(low[0], bottom, top)
        edges[1][one, :] = jnp.where(low[0], top, bottom)
        edges[2][one, :] = jnp.where(low[1], right, left)
        edges[3][one, :] = jnp.where(low[1], left, right)


def read_halo(came, halo):
    for axis, name in enumerate(("ty", "tx")):
        low = lax.rem(lax.axis_index(name), 2) == 0
        a, b = came[2 * axis][...], came[2 * axis + 1][...]
        halo[2 * axis][...] = jnp.where(low, b, a)
        halo[2 * axis + 1][...] = jnp.where(low, a, b)


def unpack(refs, *counts):
    out = []
    for count in counts:
        out.append(refs[0] if count is None else refs[:count])
        refs = refs[1 if count is None else count :]
    assert not refs
    return out


def find_slots(count_ref, owner_ref, offset_ref, slot_ref):
    slots = owner_ref.shape[0]
    across = lax.axis_size("tx")
    row_start = lax.axis_index("ty") * across
    column = lax.axis_index("tx")
    order = positions(across)
    for i in range(across):
        capture = row_start + jnp.bitwise_xor(column, order[i])
        row = col = live = jnp.int32(0)
        for t in range(slots):
            hit = jnp.where((owner_ref[t, capture] == column) & (t < count_ref[capture]), 1, 0)
            row += hit * offset_ref[t, 0, capture]
            col += hit * offset_ref[t, 1, capture]
            live += hit
        slot_ref[i, 0] = row
        slot_ref[i, 1] = col
        slot_ref[i, 2] = live


def fields_kernel(*refs):
    given, results, edges, slot_ref, kept, made, sems = unpack(refs, 8, 8, 4, None, 8, 8, None)
    uppers, lowers, fields, pupils = unpack(made, 2, 2, 2, 2)
    copies = [pltpu.make_async_copy(a, b, sems.at[i]) for i, (a, b) in enumerate(zip(given, kept))]
    for copy in copies:
        copy.start()
    for copy in copies[:3]:
        copy.wait()
    count_ref, owner_ref, offset_ref, v_ref, mask_ref, tab_ref, measured_ref, swap_ref = kept
    slots, across = owner_ref.shape[0], lax.axis_size("tx")
    find_slots(count_ref, owner_ref, offset_ref, slot_ref)
    for copy in copies[3:]:
        copy.wait()
    assert len(copies) == len(given)
    part = across // 2
    count = part // 2
    rows = uppers[0].shape[1]
    mask = mask_ref[...].astype(F32)
    side = mask.shape[0]
    highest = lax.Precision.HIGHEST
    swap = swap_ref[...]
    image = jnp.dot(swap, measured_ref[0], precision=highest, preferred_element_type=F32)
    data = lax.dot_general(
        image, swap, (((1,), (1,)), ((), ())), precision=highest, preferred_element_type=F32
    )
    jobs = []
    for y, z, i in groups(count):
        at, base = z * count + i, y * part + z * count + i

        def pupil(y=y, at=at, base=base):
            x = pltpu.roll(mask, lax.rem(slot_ref[base, 0], side), 0)
            x = pltpu.roll(x, lax.rem(slot_ref[base, 1], side), 1)
            pupils[y][at] = x
            return x

        def take(re, im, y=y, z=z, i=i, at=at, base=base):
            live = slot_ref[base, 2].astype(F32)
            re, im = re * live, im * live
            fields[y][at, 0] = 2.0 * re
            fields[y][at, 1] = 2.0 * im
            image = re * re + im * im
            if base == 0:
                image = image - data
            uppers[y][at] = image[:rows]
            lowers[z][y * count + i] = image[rows:]
            for k, j in ((y, at), (2 + z, y * count + i), (4 + y, at), (6 + y, at)):
                copy = pltpu.make_async_copy(made[k].at[j], results[k].at[j], sems.at[len(copies)])
                copy.start()
                copies.append(copy)

        jobs.append((pupil, where(slot_ref, base), take))
    to_images(jobs, v_ref, tab_ref)
    write_edges(v_ref, edges)
    for copy in copies[len(given) :]:
        copy.wait()


def groups(count):
    return [(y, z, i) for y, z in ((1, 0), (1, 1), (0, 1), (0, 0)) for i in range(count)]


def deposit_images(which, slot_ref, image_at, fields, pupils, tab_ref, acc_ref):
    count = fields[0].shape[0] // 2
    jobs = []
    for y, z, i in [(y, z, i) for y, z in which for i in range(count)]:
        at = z * count + i

        def images(y=y, z=z, i=i, at=at):
            image = image_at(y, z, i)
            return fields[y][at, 0] * image, fields[y][at, 1] * image

        def pupil(y=y, at=at):
            return pupils[y][at]

        jobs.append((pupil, where(slot_ref, 2 * y * count + at), images))
    from_images(jobs, acc_ref, tab_ref)


def linear_kernel(which, slot_ref, v_ref, tab_ref, *refs):
    pupils, fields, refs = refs[:2], refs[2:4], refs[4:]
    count = fields[0].shape[0] // 2
    if which is FAR:
        uppers, lowers = refs[-4:-2], refs[-2:]
        skip = count
    else:
        came, (upper, lower) = refs[:2], refs[-2:]
        uppers, lowers = (upper, None), (lower, None)
        upper[count:] = came[0][...]
        lower[count:] = came[1][...]
        skip = 0
    rows = uppers[0].shape[1]
    jobs = []
    for y, z, i in groups(count):
        if (y, z) not in which:
            continue
        at = z * count + i

        def take(re, im, y=y, z=z, i=i, at=at):
            image = fields[y][at, 0] * re + fields[y][at, 1] * im
            uppers[y][at if y else at - skip] = image[:rows]
            lowers[z][y * count + i - (0 if z else skip)] = image[rows:]

        def pupil(y=y, at=at):
            return pupils[y][at]

        jobs.append((pupil, where(slot_ref, 2 * y * count + at), take))
    to_images(jobs, v_ref, tab_ref)


def one_image(firsts, seconds, count):
    rows = firsts[0].shape[2] - firsts[0].shape[1]

    def image(y, z, i):
        return jnp.concatenate(
            [firsts[y][z * count + i], seconds[z][y * count + i, :rows, :]], 0
        )

    return image


def adjoint_kernel(slot_ref, start_ref, tab_ref, *refs):
    pupils, fields, firsts, seconds, acc_ref = unpack(refs, 2, 2, 2, 2, None)
    acc_ref[...] = start_ref[...]
    image = one_image(firsts, seconds, fields[0].shape[0] // 2)
    deposit_images(NEAR, slot_ref, image, fields, pupils, tab_ref, acc_ref)


def turn_kernel(sign, slot_ref, part_ref, tab_ref, *refs):
    pupils, fields, firsts, seconds, (out_ref, sum_ref), edges = unpack(refs, 2, 2, 2, 2, 2, 4)
    out_ref[...] = part_ref[...]
    image = one_image(firsts, seconds, fields[0].shape[0] // 2)
    deposit_images(FAR, slot_ref, image, fields, pupils, tab_ref, out_ref)
    found = jnp.zeros((8, 128), F32)
    if sign < 0:
        for part in (0, 1):
            for at in range(0, out_ref.shape[1], ROWS):
                value = -out_ref[part, at : at + ROWS, :]
                out_ref[part, at : at + ROWS, :] = value
                found += tiles(value * value)
    sum_ref[...] = found
    write_edges(out_ref, edges)


def bend_kernel(v_ref, *refs):
    came, refs = refs[:4], refs[4:]
    norm_ref, refs = (refs[0], refs[1:]) if len(refs) == 8 else (None, refs)
    (bent_ref, sums_ref), halo, cols_ref = unpack(refs, 2, 4, None)
    read_halo(came, halo)
    side_columns(halo[2], halo[3], cols_ref)
    found = jnp.zeros((8, 128), F32)
    for part in (0, 1):
        for at in range(0, v_ref.shape[1], ROWS):
            here, bent = laplace_rows(v_ref, halo, cols_ref, part, at, ROWS)
            bent = REG * bent
            bent_ref[part, at : at + ROWS, :] = bent
            found += tiles(here * bent)
    sums_ref[:, 128:] = found
    sums_ref[:, :128] = found if norm_ref is None else norm_ref[...]


def step_size(sums_ref):
    return total(sums_ref[:, :128]) / total(sums_ref[:, 128:])


def residual_kernel(r0_ref, q0_ref, sums_ref, *refs):
    halo_r, halo_q, (r1_ref, bent_ref, found_ref), halo, cols_ref = unpack(refs, 4, 4, 3, 4, None)
    alpha = step_size(sums_ref)
    read_halo([a[...] - alpha * b[...] for a, b in zip(halo_r, halo_q)], halo)
    side_columns(halo[2], halo[3], cols_ref)
    sums = [jnp.zeros((8, 128), F32) for _ in range(2)]
    for part in (0, 1):
        for at in range(0, r0_ref.shape[1], ROWS):
            span = slice(at, at + ROWS)
            r1_ref[part, span, :] = r0_ref[part, span, :] - alpha * q0_ref[part, span, :]
        for at in range(0, r0_ref.shape[1], ROWS):
            span = slice(at, at + ROWS)
            here, bent = laplace_rows(r1_ref, halo, cols_ref, part, at, ROWS)
            bent = REG * bent
            bent_ref[part, span, :] = bent
            sums[0] += tiles(here * here)
            sums[1] += tiles(here * bent)
    found_ref[:, :128] = sums[0]
    found_ref[:, 128:] = sums[1]


def last_kernel(which, slot_ref, start_ref, tab_ref, sums_ref, *refs):
    pupils, fields, first0, second0, firstq, secondq, acc_ref = unpack(
        refs, 2, 2, 2, 2, 2, 2, None
    )
    acc_ref[...] = start_ref[...]
    alpha = step_size(sums_ref)
    count = fields[0].shape[0] // 2
    a, b = one_image(first0, second0, count), one_image(firstq, secondq, count)
    deposit_images(
        which, slot_ref, lambda *at: a(*at) - alpha * b(*at), fields, pupils, tab_ref, acc_ref
    )


def norm_kernel(rows, count, *refs):
    sums_ref, refs = (refs[0], refs[1:]) if count == 2 else (None, refs)
    w0, refs = refs[:4], refs[4:]
    wq, out_ref = (refs[:4], refs[4]) if count == 2 else (None, refs[0])
    alpha = step_size(sums_ref) if count == 2 else None

    def body(i, acc):
        for j in range(4):
            w = w0[j][i] if j < 2 else w0[j][i, :rows, :]
            if wq:
                w = w - alpha * (wq[j][i] if j < 2 else wq[j][i, :rows, :])
            acc += tiles(w * w)
        return acc

    part = w0[0].shape[0]
    squares = lax.fori_loop(0, part, body, jnp.zeros((8, 128), F32))
    came = jnp.zeros((8, 256), F32)
    for ref in (wq or w0)[2:]:
        for i in range(part):
            came += ref[i, rows:, :]
    out_ref[:, :128] = came[:, :128]
    out_ref[:, 128:] = came[:, 128:] + squares


def finish_kernel(r0_ref, r1_ref, q0_ref, acc_ref, sums_ref, later_ref, *refs):
    results, made, sems = unpack(refs, 2, 2, None)
    step_ref, res_ref = made
    alpha = step_size(sums_ref)
    norm1 = total(later_ref[:, :128])
    beta = norm1 / total(sums_ref[:, :128])
    alpha1 = norm1 / (total(later_ref[:, 128:]) - beta * norm1 / alpha)
    copies = []
    for part in (0, 1):
        for at in range(0, r0_ref.shape[1], ROWS):
            span = (part, slice(at, at + ROWS))
            r0, r1 = r0_ref[span], r1_ref[span]
            step_ref[span] = alpha * r0 + alpha1 * (r1 + beta * r0)
            res_ref[span] = r1 - alpha1 * (acc_ref[span] + beta * q0_ref[span])
            for k in (0, 1):
                copy = pltpu.make_async_copy(
                    made[k].at[part, pl.ds(at, ROWS)],
                    results[k].at[part, pl.ds(at, ROWS)],
                    sems.at[len(copies)],
                )
                copy.start()
                copies.append(copy)
    for copy in copies:
        copy.wait()


def call(
    kernel, name, out, operands, smem=0, scratch=(), flops=0, smem_out=False, hbm=0, hbm_out=0,
    vmem=28,
):
    out_specs = [pl.BlockSpec(memory_space=pl.ANY)] * hbm_out + [VMEM] * (len(out) - hbm_out)
    if smem_out:
        out_specs[-1] = SMEM
    cost = pl.CostEstimate(
        flops=flops,
        bytes_accessed=sum(x.size * x.dtype.itemsize for x in list(operands) + list(out)),
        transcendentals=0,
    )
    in_specs = [pl.BlockSpec(memory_space=pl.ANY)] * hbm + [SMEM] * smem
    return list(
        pl.pallas_call(
            kernel,
            out_shape=out,
            in_specs=in_specs + [VMEM] * (len(operands) - len(in_specs)),
            out_specs=out_specs,
            scratch_shapes=list(scratch),
            compiler_params=pltpu.CompilerParams(vmem_limit_bytes=vmem << 20),
            cost_estimate=cost,
            name=name,
        )(*operands)
    )


def shift(x, axis, by):
    size = lax.axis_size(axis)
    pairs = [(i, i + by) for i in range(size) if 0 <= i + by < size]
    return lax.ppermute(x, axis, pairs)


def exchange(x, axis, bit):
    return lax.ppermute(x, axis, [(i, i ^ bit) for i in range(lax.axis_size(axis))])


def swap_edges(edges, axis):
    size = lax.axis_size(axis)
    out = []
    for begin, edge in enumerate(edges):
        pairs = [(i, i + 1) for i in range(begin, size - 1, 2)]
        out.append(lax.ppermute(edge, axis, pairs + [(j, i) for i, j in pairs]))
    return out


def swapped(edges):
    return swap_edges(edges[:2], "ty"), swap_edges(edges[2:], "tx")


def wait(x, done):
    return lax.optimization_barrier((x, done))


def all_bits(axis):
    return [1 << b for b in range(lax.axis_size(axis).bit_length() - 1)]


def positions(across):
    count = across.bit_length() - 1
    return [sum(((i >> b) & 1) << (count - 1 - b) for b in range(count)) for i in range(across)]


def sum_over(x, axis, bits):
    for bit in bits:
        x = x + exchange(x, axis, bit)
    return x


def scatter(low, high, bits, first, second):
    low, first = wait(low, first)
    x = (low + exchange(high, "tx", bits[0])).reshape((2,) * (len(bits) - 1) + low.shape[1:])
    for axis, bit in enumerate(bits[1:]):
        low, high = jnp.split(x, 2, axis)
        if axis == 0:
            low, second = wait(low, second)
        x = low + exchange(high, "tx", bit)
    return x, first, second


def gather(x, bits):
    shape = x.shape[-2:]
    for axis in range(len(bits) - 2, -1, -1):
        x = jnp.concatenate([x, exchange(x, "tx", bits[axis + 1])], axis)
    low = x.reshape((-1,) + shape)
    return low, exchange(low, "tx", bits[0])


def reduced(uppers, lowers, first, second, finish):
    bits = all_bits("tx")
    other = [bits[1], bits[0]] + bits[2:]
    upper, first, second = scatter(
        uppers[0], uppers[1], bits, first, second
    )
    lower, first, second = scatter(lowers[0], lowers[1], other, first, second)
    halo = first + second
    done, extra = finish(halo)
    if extra is not None:
        extra = extra.reshape(lower.shape[:-2] + extra.shape)
        lower = jnp.concatenate([lower, extra], -2)
    else:
        lower, done = wait(lower, done)
    return list(gather(upper, bits) + gather(lower, other)), done, halo


def on_device(spectrum, measured, pupil_mask, led_count, led_owner, led_offset):
    side = pupil_mask.shape[0]
    across = lax.axis_size("tx")
    part = across // 2
    slots = led_owner.shape[1]
    rows = side // 2
    tab = jnp.asarray(dft_tables(side))
    swap = np.zeros((side, side), np.float32)
    swap[np.arange(side), np.r_[0:side:2, 1:side:2]] = 1.0

    field_t = jax.ShapeDtypeStruct((part, 2, side, side), F32)
    pupil_t = jax.ShapeDtypeStruct((part, side, side), F32)
    image_t = [jax.ShapeDtypeStruct((part, n, side), F32) for n in (rows, side - rows)]
    half_t = [jax.ShapeDtypeStruct((part // 2,) + t.shape[1:], F32) for t in image_t]
    slot_t = jax.ShapeDtypeStruct((across, 4), jnp.int32)
    tile_t = jax.ShapeDtypeStruct(spectrum.shape, F32)
    sum_t = jax.ShapeDtypeStruct((8, 128), F32)
    pair_t = jax.ShapeDtypeStruct((8, 256), F32)
    row_t = jax.ShapeDtypeStruct((2, spectrum.shape[2]), F32)
    col_t = jax.ShapeDtypeStruct((2, spectrum.shape[1]), F32)
    edge_t = [row_t, row_t, col_t, col_t]
    cols_s = pltpu.VMEM((spectrum.shape[1], 8), F32)
    flops = part * 8 * 3 * side**3 * 2

    given = [
        led_count, led_owner.T, jnp.transpose(led_offset, (1, 2, 0)), spectrum, pupil_mask, tab,
        measured, jnp.asarray(swap),
    ]
    made = [image_t[0]] * 2 + [image_t[1]] * 2 + [field_t] * 2 + [pupil_t] * 2
    out = call(
        fields_kernel,
        "fields",
        made + edge_t + [slot_t],
        given,
        hbm=len(given),
        hbm_out=len(made),
        vmem=60,
        scratch=[
            (pltpu.SMEM if i < 3 else pltpu.VMEM)(x.shape, x.dtype) for i, x in enumerate(given)
        ]
        + [pltpu.VMEM(t.shape, t.dtype) for t in made]
        + [pltpu.SemaphoreType.DMA((len(given) + 4 * across,))],
        flops=2 * flops,
        smem_out=True,
    )
    uppers, lowers, fields, pupils, edges, slot = (
        out[:2], out[2:4], out[4:6], out[6:8], out[8:12], out[12],
    )

    def adjoint(images, start):
        return call(
            adjoint_kernel,
            "adjoint",
            [tile_t],
            [slot, start, tab] + pupils + fields + [images[0], images[0], images[2], images[2]],
            smem=1,
            flops=flops // 2,
        )[0]

    def turn(sign, images, start):
        out = call(
            functools.partial(turn_kernel, sign),
            "turn",
            [tile_t, sum_t] + edge_t,
            [slot, start, tab] + pupils + fields + images,
            smem=1,
            flops=3 * flops // 2,
        )
        return out[0], out[1], out[2:6]

    def linear(values, halo, *before):
        out = call(
            functools.partial(linear_kernel, FAR),
            "linear",
            [half_t[0], image_t[0], half_t[1], image_t[1]],
            [slot, values, tab] + pupils + fields + list(before),
            smem=1,
            flops=3 * flops // 2,
        )
        came, halo = wait([out[0], out[2]], halo)
        near = call(
            functools.partial(linear_kernel, NEAR),
            "linear_rest",
            image_t,
            [slot, values, tab] + pupils + fields + came,
            smem=1,
            flops=flops // 2,
        )
        return [near[0], out[1]], [near[1], out[3]], halo

    def bend(values, halo, norm=()):
        return call(
            bend_kernel,
            "bend",
            [tile_t, pair_t],
            [values] + halo + list(norm),
            scratch=[pltpu.VMEM(t.shape, F32) for t in edge_t] + [cols_s],
        )

    def norms(*operands):
        return call(
            functools.partial(norm_kernel, side - rows, len(operands) // 4),
            "norm",
            [pair_t],
            list(operands),
        )[0]

    first, second = all_bits("ty")[:1], all_bits("ty")[1:]
    images, bent, _ = reduced(
        uppers, lowers, *swapped(edges), lambda halo: (bend(spectrum, halo)[0], None)
    )
    r0, norm0, edges = turn(-1.0, images, adjoint(images, bent))
    above, beside = swapped(edges)
    uppers, lowers, above = linear(r0, above)
    images0, bent, halo_r = reduced(
        uppers, lowers, above, beside, lambda halo: bend(r0, halo, [norm0])
    )

    start = adjoint(images0, bent)
    waited, start = wait(images0, start)
    sums = sum_over(norms(*waited), "ty", first)
    q0, _, edges = turn(1.0, images0, start)
    above, beside = swapped(edges)
    uppers, lowers, above = linear(q0, above, sums)
    sums = sum_over(sums, "ty", second)
    (uppers[1], lowers[1]), sums = wait((uppers[1], lowers[1]), sums)

    def residual(halo_q):
        r1, bent, later = call(
            residual_kernel,
            "residual",
            [tile_t, tile_t, pair_t],
            [r0, q0, sums] + halo_r + halo_q,
            scratch=[pltpu.VMEM(t.shape, F32) for t in edge_t] + [cols_s],
        )
        return (r1, bent), later

    images1, (r1, bent), _ = reduced(uppers, lowers, above, beside, residual)
    def last(which, acc, w0, wq):
        return call(
            functools.partial(last_kernel, which),
            "last",
            [tile_t],
            [slot, acc, tab, sums] + pupils + fields + w0 + wq,
            smem=1,
            flops=len(which) * flops // 2,
        )[0]

    early0, early1 = [[w[0], w[0], w[2], w[2]] for w in (images0, images1)]
    acc = last(NEAR, bent, early0, early1)
    waited, acc = wait(images1, acc)
    later = sum_over(norms(sums, *images0, *waited), "ty", first + second)
    acc = last(FAR[:2], acc, images0, images1)
    acc = last(FAR[2:], acc, images0, images1)
    return tuple(
        call(
            finish_kernel,
            "finish",
            [tile_t, tile_t],
            [r0, r1, q0, acc, sums, later],
            hbm_out=2,
            scratch=[
                pltpu.VMEM(tile_t.shape, F32),
                pltpu.VMEM(tile_t.shape, F32),
                pltpu.SemaphoreType.DMA((4 * (spectrum.shape[1] // ROWS),)),
            ],
        )
    )


def solution(mesh):
    placed = (P(None, "ty", "tx"), P(("ty", "tx"), None, None), P(), P(), P(), P())
    return jax.shard_map(
        on_device,
        mesh=mesh,
        in_specs=placed,
        out_specs=(P(None, "ty", "tx"), P(None, "ty", "tx")),
        check_vma=False,
    )
```

```python
import functools

import jax
import jax.numpy as jnp
import ml_dtypes
import numpy as np
from jax import lax
from jax.experimental import pallas as pl
from jax.experimental.pallas import tpu as pltpu
from jax.sharding import PartitionSpec as P

REG = 0.5
ROWS = 64
NEAR, FAR = ((0, 0),), ((0, 1), (1, 0), (1, 1))
F32 = jnp.float32
BF16 = jnp.bfloat16
VMEM = pl.BlockSpec(memory_space=pltpu.VMEM)
SMEM = pl.BlockSpec(memory_space=pltpu.SMEM)


def dft_tables(side):
    half = side // 2
    m = np.arange(half)[:, None]
    k = np.arange(half)[None, :]
    out = []
    for q in (0, 1):
        angle = 2 * np.pi * (((2 * m + q) * k) % side) / side
        cos, sin = np.cos(angle) / np.sqrt(side), np.sin(angle) / np.sqrt(side)
        mat = np.block([[cos.T, sin.T], [-sin.T, cos.T]])
        for each in (mat, mat.T):
            high = each.astype(ml_dtypes.bfloat16)
            low = (each - high.astype(np.float64)).astype(ml_dtypes.bfloat16)
            out += [high, low]
    return np.stack(out)


def split(x):
    high = x.astype(BF16)
    return high, (x - high.astype(F32)).astype(BF16)


def rmul(parts, tab_ref, at):
    a, b = parts
    high, low = tab_ref[at], tab_ref[at + 1]
    return jnp.dot(
        jnp.concatenate([a, b, a], 1),
        jnp.concatenate([high, high, low], 0),
        preferred_element_type=F32,
    )


def lmul(tab_ref, at, parts):
    a, b = parts
    high, low = tab_ref[at], tab_ref[at + 1]
    return jnp.dot(
        jnp.concatenate([high, high, low], 1),
        jnp.concatenate([a, b, a], 0),
        preferred_element_type=F32,
    )


def pipelined(count, stages):
    state = {}

    def run(stage, k):
        if k < count:
            state[k] = stages[stage](k, state.get(k))

    run(0, 0)
    run(1, 0)
    run(0, 1)
    for k in range(count):
        run(1, k + 1)
        run(2, k)
        run(3, k)
        run(0, k + 2)
        run(4, k)
        del state[k]


def masks(start, side):
    rows = lax.broadcasted_iota(jnp.int32, (side, side // 2), 0) >= start[0]
    lane = lax.broadcasted_iota(jnp.int32, (side, side // 2), 1)
    return rows, [lane + j * (side // 2) >= start[1] for j in (0, 1)]


def extract(v_ref, part, start, side):
    half = side // 2
    rows, cols = masks(start, side)
    out = []
    for j in (0, 1):
        near, far = slice(j * half, (j + 1) * half), slice(side + j * half, side + (j + 1) * half)
        top = jnp.where(cols[j], v_ref[part, :side, near], v_ref[part, :side, far])
        low = jnp.where(cols[j], v_ref[part, side:, near], v_ref[part, side:, far])
        out.append(jnp.where(rows, top, low))
    return out


def deposit(acc_ref, part, start, halves, side):
    half = side // 2
    rows, cols = masks(start, side)
    for j, x in enumerate(halves):
        top, low = jnp.where(rows, x, 0.0), jnp.where(rows, 0.0, x)
        for at, value in ((slice(0, side), top), (slice(side, 2 * side), low)):
            near = (part, at, slice(j * half, (j + 1) * half))
            far = (part, at, slice(side + j * half, side + (j + 1) * half))
            acc_ref[near] = acc_ref[near] + jnp.where(cols[j], value, 0.0)
            acc_ref[far] = acc_ref[far] + jnp.where(cols[j], 0.0, value)


def to_images(jobs, v_ref, tab_ref):
    def cut(k, _):
        pupil, start, _ = jobs[k]
        pupil, start = pupil(), start()
        side = pupil.shape[0]
        half = side // 2
        plus, minus = [], []
        for part in (0, 1):
            x0, x1 = extract(v_ref, part, start, side)
            x0, x1 = x0 * pupil[:, :half], x1 * pupil[:, half:]
            plus.append(x0 + x1)
            minus.append(x0 - x1)
        return split(jnp.concatenate(plus, 1)), split(jnp.concatenate(minus, 1))

    def columns(k, x):
        return rmul(x[0], tab_ref, 0), rmul(x[1], tab_ref, 4)

    def fold(k, x):
        even, odd = x
        half = even.shape[1] // 2
        re = jnp.concatenate([even[:, :half], odd[:, :half]], 1)
        im = jnp.concatenate([even[:, half:], odd[:, half:]], 1)
        top = jnp.concatenate([re[:half] + re[half:], im[:half] + im[half:]], 0)
        low = jnp.concatenate([re[:half] - re[half:], im[:half] - im[half:]], 0)
        return split(top), split(low)

    def rows(k, x):
        return lmul(tab_ref, 2, x[0]), lmul(tab_ref, 6, x[1])

    def give(k, x):
        even, odd = x
        half = even.shape[0] // 2
        jobs[k][2](
            jnp.concatenate([even[:half], odd[:half]], 0),
            jnp.concatenate([even[half:], odd[half:]], 0),
        )

    pipelined(len(jobs), (cut, columns, fold, rows, give))


def from_images(jobs, acc_ref, tab_ref):
    def cut(k, _):
        re, im = jobs[k][2]()
        half = re.shape[0] // 2
        even = jnp.concatenate([re[:half], im[:half]], 0)
        odd = jnp.concatenate([re[half:], im[half:]], 0)
        return split(even), split(odd)

    def rows(k, x):
        return lmul(tab_ref, 0, x[0]), lmul(tab_ref, 4, x[1])

    def fold(k, x):
        even, odd = x
        half = even.shape[0] // 2
        top, low = even + odd, even - odd
        re = jnp.concatenate([top[:half], low[:half]], 0)
        im = jnp.concatenate([top[half:], low[half:]], 0)
        return (
            split(jnp.concatenate([re[:, :half], im[:, :half]], 1)),
            split(jnp.concatenate([re[:, half:], im[:, half:]], 1)),
        )

    def columns(k, x):
        return rmul(x[0], tab_ref, 2), rmul(x[1], tab_ref, 6)

    def give(k, x):
        even, odd = x
        pupil, start = jobs[k][0](), jobs[k][1]()
        half = pupil.shape[0] // 2
        p0, p1 = pupil[:, :half], pupil[:, half:]
        left, right = even + odd, even - odd
        for part in (0, 1):
            at = slice(part * half, (part + 1) * half)
            deposit(acc_ref, part, start, (left[:, at] * p0, right[:, at] * p1), 2 * half)

    pipelined(len(jobs), (cut, rows, fold, columns, give))


def where(slot_ref, i):
    return lambda: (slot_ref[i, 0], slot_ref[i, 1])


def tiles(x):
    rows, cols = x.shape
    x = jnp.sum(x.reshape(rows // 8, 8, cols), 0)
    return sum(x[:, i * 128 : (i + 1) * 128] for i in range(cols // 128))


def total(tile):
    return jnp.sum(jnp.sum(tile, 0, keepdims=True), 1, keepdims=True)


def side_columns(left_ref, right_ref, cols_ref):
    size = left_ref.shape[1]
    rows = jnp.concatenate([left_ref[...], right_ref[...], jnp.zeros((4, size), F32)], 0)
    cols_ref[...] = jnp.transpose(rows)


def laplace_rows(v_ref, halo, cols_ref, part, at, count):
    top_ref, bottom_ref = halo[:2]
    rows, cols = v_ref.shape[1:]
    here = v_ref[part, at : at + count, :]
    up = (
        jnp.concatenate([top_ref[part : part + 1, :], v_ref[part, : count - 1, :]], 0)
        if at == 0
        else v_ref[part, at - 1 : at + count - 1, :]
    )
    down = (
        jnp.concatenate([v_ref[part, at + 1 :, :], bottom_ref[part : part + 1, :]], 0)
        if at + count == rows
        else v_ref[part, at + 1 : at + count + 1, :]
    )
    lane = lax.broadcasted_iota(jnp.int32, (count, cols), 1)
    span = slice(at, at + count)
    before = jnp.where(lane == 0, cols_ref[span, part : part + 1], pltpu.roll(here, 1, 1))
    after = jnp.where(
        lane == cols - 1, cols_ref[span, 2 + part : 3 + part], pltpu.roll(here, cols - 1, 1)
    )
    return here, 4.0 * here - (up + down + before + after)


def write_edges(v_ref, edges):
    rows, cols = v_ref.shape[1:]
    low = [lax.rem(lax.axis_index(axis), 2) == 0 for axis in ("ty", "tx")]
    for part in (0, 1):
        one = slice(part, part + 1)
        left = jnp.transpose(v_ref[part, :, :128])[:1]
        right = jnp.transpose(v_ref[part, :, cols - 128 :])[127:128]
        top, bottom = v_ref[part, 0:1, :], v_ref[part, rows - 1 : rows, :]
        edges[0][one, :] = jnp.where(low[0], bottom, top)
        edges[1][one, :] = jnp.where(low[0], top, bottom)
        edges[2][one, :] = jnp.where(low[1], right, left)
        edges[3][one, :] = jnp.where(low[1], left, right)


def read_halo(came, halo):
    for axis, name in enumerate(("ty", "tx")):
        low = lax.rem(lax.axis_index(name), 2) == 0
        a, b = came[2 * axis][...], came[2 * axis + 1][...]
        halo[2 * axis][...] = jnp.where(low, b, a)
        halo[2 * axis + 1][...] = jnp.where(low, a, b)


def unpack(refs, *counts):
    out = []
    for count in counts:
        out.append(refs[0] if count is None else refs[:count])
        refs = refs[1 if count is None else count :]
    assert not refs
    return out


def find_slots(count_ref, owner_ref, offset_ref, slot_ref):
    slots = owner_ref.shape[0]
    across = lax.axis_size("tx")
    row_start = lax.axis_index("ty") * across
    column = lax.axis_index("tx")
    order = positions(across)
    for i in range(across):
        capture = row_start + jnp.bitwise_xor(column, order[i])
        row = col = live = jnp.int32(0)
        for t in range(slots):
            hit = jnp.where((owner_ref[t, capture] == column) & (t < count_ref[capture]), 1, 0)
            row += hit * offset_ref[t, 0, capture]
            col += hit * offset_ref[t, 1, capture]
            live += hit
        slot_ref[i, 0] = row
        slot_ref[i, 1] = col
        slot_ref[i, 2] = live


def fields_kernel(*refs):
    given, results, edges, slot_ref, kept, made, sems = unpack(refs, 8, 8, 4, None, 8, 8, None)
    uppers, lowers, fields, pupils = unpack(made, 2, 2, 2, 2)
    copies = [pltpu.make_async_copy(a, b, sems.at[i]) for i, (a, b) in enumerate(zip(given, kept))]
    for copy in copies:
        copy.start()
    for copy in copies[:3]:
        copy.wait()
    count_ref, owner_ref, offset_ref, v_ref, mask_ref, tab_ref, measured_ref, swap_ref = kept
    slots, across = owner_ref.shape[0], lax.axis_size("tx")
    find_slots(count_ref, owner_ref, offset_ref, slot_ref)
    for copy in copies[3:]:
        copy.wait()
    assert len(copies) == len(given)
    part = across // 2
    count = part // 2
    rows = uppers[0].shape[1]
    mask = mask_ref[...].astype(F32)
    side = mask.shape[0]
    highest = lax.Precision.HIGHEST
    swap = swap_ref[...]
    image = jnp.dot(swap, measured_ref[0], precision=highest, preferred_element_type=F32)
    data = lax.dot_general(
        image, swap, (((1,), (1,)), ((), ())), precision=highest, preferred_element_type=F32
    )
    jobs = []
    for y, z, i in groups(count):
        at, base = z * count + i, y * part + z * count + i

        def pupil(y=y, at=at, base=base):
            x = pltpu.roll(mask, lax.rem(slot_ref[base, 0], side), 0)
            x = pltpu.roll(x, lax.rem(slot_ref[base, 1], side), 1)
            pupils[y][at] = x
            return x

        def take(re, im, y=y, z=z, i=i, at=at, base=base):
            live = slot_ref[base, 2].astype(F32)
            re, im = re * live, im * live
            fields[y][at, 0] = 2.0 * re
            fields[y][at, 1] = 2.0 * im
            image = re * re + im * im
            if base == 0:
                image = image - data
            uppers[y][at] = image[:rows]
            lowers[z][y * count + i] = image[rows:]
            for k, j in ((y, at), (2 + z, y * count + i), (4 + y, at), (6 + y, at)):
                copy = pltpu.make_async_copy(made[k].at[j], results[k].at[j], sems.at[len(copies)])
                copy.start()
                copies.append(copy)

        jobs.append((pupil, where(slot_ref, base), take))
    to_images(jobs, v_ref, tab_ref)
    write_edges(v_ref, edges)
    for copy in copies[len(given) :]:
        copy.wait()


def groups(count):
    return [(y, z, i) for y, z in ((1, 0), (1, 1), (0, 1), (0, 0)) for i in range(count)]


def deposit_images(which, slot_ref, image_at, fields, pupils, tab_ref, acc_ref):
    count = fields[0].shape[0] // 2
    jobs = []
    for y, z, i in [(y, z, i) for y, z in which for i in range(count)]:
        at = z * count + i

        def images(y=y, z=z, i=i, at=at):
            image = image_at(y, z, i)
            return fields[y][at, 0] * image, fields[y][at, 1] * image

        def pupil(y=y, at=at):
            return pupils[y][at]

        jobs.append((pupil, where(slot_ref, 2 * y * count + at), images))
    from_images(jobs, acc_ref, tab_ref)


def linear_kernel(which, slot_ref, v_ref, tab_ref, *refs):
    pupils, fields, refs = refs[:2], refs[2:4], refs[4:]
    count = fields[0].shape[0] // 2
    if which is FAR:
        uppers, lowers = refs[-4:-2], refs[-2:]
        skip = count
    else:
        came, (upper, lower) = refs[:2], refs[-2:]
        uppers, lowers = (upper, None), (lower, None)
        upper[count:] = came[0][...]
        lower[count:] = came[1][...]
        skip = 0
    rows = uppers[0].shape[1]
    jobs = []
    for y, z, i in groups(count):
        if (y, z) not in which:
            continue
        at = z * count + i

        def take(re, im, y=y, z=z, i=i, at=at):
            image = fields[y][at, 0] * re + fields[y][at, 1] * im
            uppers[y][at if y else at - skip] = image[:rows]
            lowers[z][y * count + i - (0 if z else skip)] = image[rows:]

        def pupil(y=y, at=at):
            return pupils[y][at]

        jobs.append((pupil, where(slot_ref, 2 * y * count + at), take))
    to_images(jobs, v_ref, tab_ref)


def one_image(firsts, seconds, count):
    rows = firsts[0].shape[2] - firsts[0].shape[1]

    def image(y, z, i):
        return jnp.concatenate(
            [firsts[y][z * count + i], seconds[z][y * count + i, :rows, :]], 0
        )

    return image


def adjoint_kernel(slot_ref, start_ref, tab_ref, *refs):
    pupils, fields, firsts, seconds, acc_ref = unpack(refs, 2, 2, 2, 2, None)
    acc_ref[...] = start_ref[...]
    image = one_image(firsts, seconds, fields[0].shape[0] // 2)
    deposit_images(NEAR, slot_ref, image, fields, pupils, tab_ref, acc_ref)


def turn_kernel(sign, slot_ref, part_ref, tab_ref, *refs):
    pupils, fields, firsts, seconds, (out_ref, sum_ref), edges = unpack(refs, 2, 2, 2, 2, 2, 4)
    out_ref[...] = part_ref[...]
    image = one_image(firsts, seconds, fields[0].shape[0] // 2)
    deposit_images(FAR, slot_ref, image, fields, pupils, tab_ref, out_ref)
    found = jnp.zeros((8, 128), F32)
    if sign < 0:
        for part in (0, 1):
            for at in range(0, out_ref.shape[1], ROWS):
                value = -out_ref[part, at : at + ROWS, :]
                out_ref[part, at : at + ROWS, :] = value
                found += tiles(value * value)
    sum_ref[...] = found
    write_edges(out_ref, edges)


def bend_kernel(v_ref, *refs):
    came, refs = refs[:4], refs[4:]
    norm_ref, refs = (refs[0], refs[1:]) if len(refs) == 8 else (None, refs)
    (bent_ref, sums_ref), halo, cols_ref = unpack(refs, 2, 4, None)
    read_halo(came, halo)
    side_columns(halo[2], halo[3], cols_ref)
    found = jnp.zeros((8, 128), F32)
    for part in (0, 1):
        for at in range(0, v_ref.shape[1], ROWS):
            here, bent = laplace_rows(v_ref, halo, cols_ref, part, at, ROWS)
            bent = REG * bent
            bent_ref[part, at : at + ROWS, :] = bent
            found += tiles(here * bent)
    sums_ref[:, 128:] = found
    sums_ref[:, :128] = found if norm_ref is None else norm_ref[...]


def step_size(sums_ref):
    return total(sums_ref[:, :128]) / total(sums_ref[:, 128:])


def residual_kernel(r0_ref, q0_ref, sums_ref, *refs):
    halo_r, halo_q, (r1_ref, bent_ref, found_ref), halo, cols_ref = unpack(refs, 4, 4, 3, 4, None)
    alpha = step_size(sums_ref)
    read_halo([a[...] - alpha * b[...] for a, b in zip(halo_r, halo_q)], halo)
    side_columns(halo[2], halo[3], cols_ref)
    sums = [jnp.zeros((8, 128), F32) for _ in range(2)]
    for part in (0, 1):
        for at in range(0, r0_ref.shape[1], ROWS):
            span = slice(at, at + ROWS)
            r1_ref[part, span, :] = r0_ref[part, span, :] - alpha * q0_ref[part, span, :]
        for at in range(0, r0_ref.shape[1], ROWS):
            span = slice(at, at + ROWS)
            here, bent = laplace_rows(r1_ref, halo, cols_ref, part, at, ROWS)
            bent = REG * bent
            bent_ref[part, span, :] = bent
            sums[0] += tiles(here * here)
            sums[1] += tiles(here * bent)
    found_ref[:, :128] = sums[0]
    found_ref[:, 128:] = sums[1]


def last_kernel(which, slot_ref, start_ref, tab_ref, sums_ref, *refs):
    pupils, fields, first0, second0, firstq, secondq, acc_ref = unpack(
        refs, 2, 2, 2, 2, 2, 2, None
    )
    acc_ref[...] = start_ref[...]
    alpha = step_size(sums_ref)
    count = fields[0].shape[0] // 2
    a, b = one_image(first0, second0, count), one_image(firstq, secondq, count)
    deposit_images(
        which, slot_ref, lambda *at: a(*at) - alpha * b(*at), fields, pupils, tab_ref, acc_ref
    )


def norm_kernel(rows, count, *refs):
    sums_ref, refs = (refs[0], refs[1:]) if count == 2 else (None, refs)
    w0, refs = refs[:4], refs[4:]
    wq, out_ref = (refs[:4], refs[4]) if count == 2 else (None, refs[0])
    alpha = step_size(sums_ref) if count == 2 else None

    def body(i, acc):
        for j in range(4):
            w = w0[j][i] if j < 2 else w0[j][i, :rows, :]
            if wq:
                w = w - alpha * (wq[j][i] if j < 2 else wq[j][i, :rows, :])
            acc += tiles(w * w)
        return acc

    part = w0[0].shape[0]
    squares = lax.fori_loop(0, part, body, jnp.zeros((8, 128), F32))
    came = jnp.zeros((8, 256), F32)
    for ref in (wq or w0)[2:]:
        for i in range(part):
            came += ref[i, rows:, :]
    out_ref[:, :128] = came[:, :128]
    out_ref[:, 128:] = came[:, 128:] + squares


def finish_kernel(r0_ref, r1_ref, q0_ref, acc_ref, sums_ref, later_ref, *refs):
    results, made, sems = unpack(refs, 2, 2, None)
    step_ref, res_ref = made
    alpha = step_size(sums_ref)
    norm1 = total(later_ref[:, :128])
    beta = norm1 / total(sums_ref[:, :128])
    alpha1 = norm1 / (total(later_ref[:, 128:]) - beta * norm1 / alpha)
    copies = []
    for part in (0, 1):
        for at in range(0, r0_ref.shape[1], ROWS):
            span = (part, slice(at, at + ROWS))
            r0, r1 = r0_ref[span], r1_ref[span]
            step_ref[span] = alpha * r0 + alpha1 * (r1 + beta * r0)
            res_ref[span] = r1 - alpha1 * (acc_ref[span] + beta * q0_ref[span])
            for k in (0, 1):
                copy = pltpu.make_async_copy(
                    made[k].at[part, pl.ds(at, ROWS)],
                    results[k].at[part, pl.ds(at, ROWS)],
                    sems.at[len(copies)],
                )
                copy.start()
                copies.append(copy)
    for copy in copies:
        copy.wait()


def call(
    kernel, name, out, operands, smem=0, scratch=(), flops=0, smem_out=False, hbm=0, hbm_out=0,
    vmem=28,
):
    out_specs = [pl.BlockSpec(memory_space=pl.ANY)] * hbm_out + [VMEM] * (len(out) - hbm_out)
    if smem_out:
        out_specs[-1] = SMEM
    cost = pl.CostEstimate(
        flops=flops,
        bytes_accessed=sum(x.size * x.dtype.itemsize for x in list(operands) + list(out)),
        transcendentals=0,
    )
    in_specs = [pl.BlockSpec(memory_space=pl.ANY)] * hbm + [SMEM] * smem
    return list(
        pl.pallas_call(
            kernel,
            out_shape=out,
            in_specs=in_specs + [VMEM] * (len(operands) - len(in_specs)),
            out_specs=out_specs,
            scratch_shapes=list(scratch),
            compiler_params=pltpu.CompilerParams(vmem_limit_bytes=vmem << 20),
            cost_estimate=cost,
            name=name,
        )(*operands)
    )


def shift(x, axis, by):
    size = lax.axis_size(axis)
    pairs = [(i, i + by) for i in range(size) if 0 <= i + by < size]
    return lax.ppermute(x, axis, pairs)


def exchange(x, axis, bit):
    return lax.ppermute(x, axis, [(i, i ^ bit) for i in range(lax.axis_size(axis))])


def swap_edges(edges, axis):
    size = lax.axis_size(axis)
    out = []
    for begin, edge in enumerate(edges):
        pairs = [(i, i + 1) for i in range(begin, size - 1, 2)]
        out.append(lax.ppermute(edge, axis, pairs + [(j, i) for i, j in pairs]))
    return out


def swapped(edges):
    return swap_edges(edges[:2], "ty"), swap_edges(edges[2:], "tx")


def wait(x, done):
    return lax.optimization_barrier((x, done))


def all_bits(axis):
    return [1 << b for b in range(lax.axis_size(axis).bit_length() - 1)]


def positions(across):
    count = across.bit_length() - 1
    return [sum(((i >> b) & 1) << (count - 1 - b) for b in range(count)) for i in range(across)]


def sum_over(x, axis, bits):
    for bit in bits:
        x = x + exchange(x, axis, bit)
    return x


def scatter(low, high, bits, first, second):
    low, first = wait(low, first)
    x = (low + exchange(high, "tx", bits[0])).reshape((2,) * (len(bits) - 1) + low.shape[1:])
    for axis, bit in enumerate(bits[1:]):
        low, high = jnp.split(x, 2, axis)
        if axis == 0:
            low, second = wait(low, second)
        x = low + exchange(high, "tx", bit)
    return x, first, second


def gather(x, bits):
    shape = x.shape[-2:]
    for axis in range(len(bits) - 2, -1, -1):
        x = jnp.concatenate([x, exchange(x, "tx", bits[axis + 1])], axis)
    low = x.reshape((-1,) + shape)
    return low, exchange(low, "tx", bits[0])


def reduced(uppers, lowers, first, second, finish):
    bits = all_bits("tx")
    other = [bits[1], bits[0]] + bits[2:]
    upper, first, second = scatter(
        uppers[0], uppers[1], bits, first, second
    )
    lower, first, second = scatter(lowers[0], lowers[1], other, first, second)
    halo = first + second
    done, extra = finish(halo)
    if extra is not None:
        extra = extra.reshape(lower.shape[:-2] + extra.shape)
        lower = jnp.concatenate([lower, extra], -2)
    else:
        lower, done = wait(lower, done)
    return list(gather(upper, bits) + gather(lower, other)), done, halo


def on_device(spectrum, measured, pupil_mask, led_count, led_owner, led_offset):
    side = pupil_mask.shape[0]
    across = lax.axis_size("tx")
    part = across // 2
    slots = led_owner.shape[1]
    rows = side // 2
    tab = jnp.asarray(dft_tables(side))
    swap = np.zeros((side, side), np.float32)
    swap[np.arange(side), np.r_[0:side:2, 1:side:2]] = 1.0

    field_t = jax.ShapeDtypeStruct((part, 2, side, side), F32)
    pupil_t = jax.ShapeDtypeStruct((part, side, side), F32)
    image_t = [jax.ShapeDtypeStruct((part, n, side), F32) for n in (rows, side - rows)]
    half_t = [jax.ShapeDtypeStruct((part // 2,) + t.shape[1:], F32) for t in image_t]
    slot_t = jax.ShapeDtypeStruct((across, 4), jnp.int32)
    tile_t = jax.ShapeDtypeStruct(spectrum.shape, F32)
    sum_t = jax.ShapeDtypeStruct((8, 128), F32)
    pair_t = jax.ShapeDtypeStruct((8, 256), F32)
    row_t = jax.ShapeDtypeStruct((2, spectrum.shape[2]), F32)
    col_t = jax.ShapeDtypeStruct((2, spectrum.shape[1]), F32)
    edge_t = [row_t, row_t, col_t, col_t]
    cols_s = pltpu.VMEM((spectrum.shape[1], 8), F32)
    flops = part * 8 * 3 * side**3 * 2

    given = [
        led_count, led_owner.T, jnp.transpose(led_offset, (1, 2, 0)), spectrum, pupil_mask, tab,
        measured, jnp.asarray(swap),
    ]
    made = [image_t[0]] * 2 + [image_t[1]] * 2 + [field_t] * 2 + [pupil_t] * 2
    out = call(
        fields_kernel,
        "fields",
        made + edge_t + [slot_t],
        given,
        hbm=len(given),
        hbm_out=len(made),
        vmem=60,
        scratch=[
            (pltpu.SMEM if i < 3 else pltpu.VMEM)(x.shape, x.dtype) for i, x in enumerate(given)
        ]
        + [pltpu.VMEM(t.shape, t.dtype) for t in made]
        + [pltpu.SemaphoreType.DMA((len(given) + 4 * across,))],
        flops=2 * flops,
        smem_out=True,
    )
    uppers, lowers, fields, pupils, edges, slot = (
        out[:2], out[2:4], out[4:6], out[6:8], out[8:12], out[12],
    )

    def adjoint(images, start):
        return call(
            adjoint_kernel,
            "adjoint",
            [tile_t],
            [slot, start, tab] + pupils + fields + [images[0], images[0], images[2], images[2]],
            smem=1,
            flops=flops // 2,
        )[0]

    def turn(sign, images, start):
        out = call(
            functools.partial(turn_kernel, sign),
            "turn",
            [tile_t, sum_t] + edge_t,
            [slot, start, tab] + pupils + fields + images,
            smem=1,
            flops=3 * flops // 2,
        )
        return out[0], out[1], out[2:6]

    def linear(values, halo, *before):
        out = call(
            functools.partial(linear_kernel, FAR),
            "linear",
            [half_t[0], image_t[0], half_t[1], image_t[1]],
            [slot, values, tab] + pupils + fields + list(before),
            smem=1,
            flops=3 * flops // 2,
        )
        came, halo = wait([out[0], out[2]], halo)
        near = call(
            functools.partial(linear_kernel, NEAR),
            "linear_rest",
            image_t,
            [slot, values, tab] + pupils + fields + came,
            smem=1,
            flops=flops // 2,
        )
        return [near[0], out[1]], [near[1], out[3]], halo

    def bend(values, halo, norm=()):
        return call(
            bend_kernel,
            "bend",
            [tile_t, pair_t],
            [values] + halo + list(norm),
            scratch=[pltpu.VMEM(t.shape, F32) for t in edge_t] + [cols_s],
        )

    def norms(*operands):
        return call(
            functools.partial(norm_kernel, side - rows, len(operands) // 4),
            "norm",
            [pair_t],
            list(operands),
        )[0]

    first, second = all_bits("ty")[:1], all_bits("ty")[1:]
    images, bent, _ = reduced(
        uppers, lowers, *swapped(edges), lambda halo: (bend(spectrum, halo)[0], None)
    )
    r0, norm0, edges = turn(-1.0, images, adjoint(images, bent))
    above, beside = swapped(edges)
    uppers, lowers, above = linear(r0, above)
    images0, bent, halo_r = reduced(
        uppers, lowers, above, beside, lambda halo: bend(r0, halo, [norm0])
    )

    start = adjoint(images0, bent)
    waited, start = wait(images0, start)
    sums = sum_over(norms(*waited), "ty", first)
    q0, _, edges = turn(1.0, images0, start)
    above, beside = swapped(edges)
    uppers, lowers, above = linear(q0, above, sums)
    sums = sum_over(sums, "ty", second)
    above, sums = wait(above, sums)

    def residual(halo_q):
        r1, bent, later = call(
            residual_kernel,
            "residual",
            [tile_t, tile_t, pair_t],
            [r0, q0, sums] + halo_r + halo_q,
            scratch=[pltpu.VMEM(t.shape, F32) for t in edge_t] + [cols_s],
        )
        return (r1, bent), later

    images1, (r1, bent), _ = reduced(uppers, lowers, above, beside, residual)
    def last(which, acc, w0, wq):
        return call(
            functools.partial(last_kernel, which),
            "last",
            [tile_t],
            [slot, acc, tab, sums] + pupils + fields + w0 + wq,
            smem=1,
            flops=len(which) * flops // 2,
        )[0]

    early0, early1 = [[w[0], w[0], w[2], w[2]] for w in (images0, images1)]
    acc = last(NEAR, bent, early0, early1)
    waited, acc = wait(images1, acc)
    later = sum_over(norms(sums, *images0, *waited), "ty", first + second)
    acc = last(FAR[:2], acc, images0, images1)
    acc = last(FAR[2:], acc, images0, images1)
    return tuple(
        call(
            finish_kernel,
            "finish",
            [tile_t, tile_t],
            [r0, r1, q0, acc, sums, later],
            hbm_out=2,
            scratch=[
                pltpu.VMEM(tile_t.shape, F32),
                pltpu.VMEM(tile_t.shape, F32),
                pltpu.SemaphoreType.DMA((4 * (spectrum.shape[1] // ROWS),)),
            ],
        )
    )


def solution(mesh):
    placed = (P(None, "ty", "tx"), P(("ty", "tx"), None, None), P(), P(), P(), P())
    return jax.shard_map(
        on_device,
        mesh=mesh,
        in_specs=placed,
        out_specs=(P(None, "ty", "tx"), P(None, "ty", "tx")),
        check_vma=False,
    )
```
